32 devices in a mesh: dp: 16 (over z, x, core), blk: 2 (over y).
Axes of the slice: x: 2, y: 2, z: 4, core: 2. Of those that a mesh axis runs over, the one named last changes fastest.
Arguments:
- tokens: bfloat16 [16, 1280, 768], P('dp', 'blk'), may hold values from -6 to 6
- segment_ids: int32 [16, 1280], P('dp', 'blk'), may hold values from 0 to 6, as said below
- gain_attn: float32 [768], replicated, may hold values from 0.5 to 1.5
- w_qkv: bfloat16 [768, 2304], replicated, may hold values from -0.21875 to 0.21875
- w_out: bfloat16 [768, 768], replicated, may hold values from -2.5 to 2.5
- gain_ffn: float32 [768], replicated, may hold values from 0.5 to 1.5
- w_up: bfloat16 [768, 3072], replicated, may hold values from -0.21875 to 0.21875
- w_down: bfloat16 [3072, 768], replicated, may hold values from -0.109375 to 0.109375
- cotangent: bfloat16 [16, 1280, 768], P('dp', 'blk'), may hold values from -6 to 6
Outputs:
- layer_out: float32 [16, 1280, 768], P('dp', 'blk')
- input_grad: float32 [16, 1280, 768], P('dp', 'blk')
- grad_gain_attn: float32 [768], P('dp')
- grad_qkv: float32 [768, 2304], P('dp', 'blk')
- grad_out: float32 [768, 768], P('dp', 'blk')
- grad_gain_ffn: float32 [768], P('dp')
- grad_up: float32 [768, 3072], P('dp', 'blk')
- grad_down: float32 [3072, 768], P('dp', 'blk')
The draws below stay inside these ranges and needn't reach their ends.
Inputs may be any that keep to these rules, and one draw needn't show every extreme that they name: Each sequence is packed with whole images of 197 or 577 positions, the last one cut at the sequence's end; segment_ids start at 0 and rise by one at each new image; one sequence holds only images of 197 positions.
All inputs are finite; a program needn't handle non-finite values.
Results may differ from the reference program's by a relative error of at most 0.02.
Values may be sent and summed in bfloat16 or wider, within the bound.
A program may use at most 192 MiB of HBM per device.

```python
import math
import jax
import jax.numpy as jnp
from jax import lax

D = 768
HEADS = 12
HDIM = 64
FF = 3072
IMG_SMALL = 197
IMG_LARGE = 577
LENGTH = 1280
SEQS = 16


def draw_segment_ids(key, part):
    key = jax.random.fold_in(key, 7)
    slots = LENGTH // IMG_SMALL + 2
    pick_large = jax.random.randint(key, (SEQS, slots), 0, 2)
    chosen = jax.random.randint(jax.random.fold_in(key, 11), (), 0, SEQS)
    row_index = jnp.arange(SEQS, dtype=jnp.int32)
    pick_large = jnp.where(row_index[:, None] == chosen, 0, pick_large)
    sizes_img = jnp.where(pick_large == 1, IMG_LARGE, IMG_SMALL).astype(jnp.int32)
    ends = jnp.cumsum(sizes_img, axis=1).astype(jnp.int32)
    position = jnp.arange(LENGTH, dtype=jnp.int32)
    passed = (position[None, :, None] >= ends[:, None, :]).astype(jnp.int32)
    return jnp.sum(passed, axis=2).astype(jnp.int32)


def levels(key, dims, cuts, low, top_value):
    loudness, own = 1.0, jax.random.fold_in(key, 6)
    for dim, blocks in cuts:
        heights = jnp.exp(jax.random.uniform(jax.random.fold_in(own, dim), (blocks,), jnp.float32, low / len(cuts), top_value / len(cuts)))
        loudness = loudness * jnp.repeat(heights, dims[dim] // blocks).reshape([-1 if axis == dim else 1 for axis in range(len(dims))])
    return loudness


def bell_draw(key, dims, deviation, reach, pieces=(), kind=jnp.bfloat16):
    factor_of = levels(key, dims, pieces, -0.22, 0.18) if pieces else 1.0
    array = jax.random.normal(key, dims, jnp.float32) * deviation * factor_of
    return jnp.minimum(jnp.maximum(array, -reach), reach).astype(kind)


def setup_inputs(seed: int = 0) -> dict:
    arg_keys = jax.random.split(jax.random.key(seed), 10)
    tokens = bell_draw(arg_keys[0], (SEQS, LENGTH, D), 1.0, 6.0, ((0, 16), (1, 2)))
    segment_ids = draw_segment_ids(jax.random.fold_in(arg_keys[9], 71), 0)
    gain_attn = jnp.clip(1.0 + 0.1 * jax.random.normal(arg_keys[2], (D,), jnp.float32), 0.5, 1.5)
    w_qkv = bell_draw(arg_keys[3], (D, 3 * D), D ** -0.5, 0.21875)
    w_out = bell_draw(arg_keys[4], (D, D), (max(1, D * 4 // IMG_LARGE)) ** -0.5, 2.5)
    gain_ffn = jnp.clip(1.0 + 0.1 * jax.random.normal(arg_keys[5], (D,), jnp.float32), 0.5, 1.5)
    w_up = bell_draw(arg_keys[6], (D, FF), D ** -0.5, 0.21875)
    w_down = bell_draw(arg_keys[7], (FF, D), FF ** -0.5, 0.109375)
    cotangent = bell_draw(arg_keys[8], (SEQS, LENGTH, D), 1.0, 6.0, ((0, 16), (1, 2)))
    return dict(tokens=tokens, segment_ids=segment_ids, gain_attn=gain_attn, w_qkv=w_qkv, w_out=w_out, gain_ffn=gain_ffn, w_up=w_up, w_down=w_down, cotangent=cotangent)


@jax.custom_vjp
def low(v):
    return lax.optimization_barrier(v.astype(jnp.bfloat16)).astype(jnp.float32)

@jax.custom_vjp
def low_back(v):
    return v

def low_keep(v):
    return (low(v), None)

def low_pass(kept, grad):
    return (grad,)

def back_keep(v):
    return (v, None)

def back_low(kept, grad):
    return (low(grad),)
low.defvjp(low_keep, low_pass)
low_back.defvjp(back_keep, back_low)
highest = lax.Precision.HIGHEST

def normalize(values):
    centered = values - lax.optimization_barrier(jnp.mean(values, -1, keepdims=True))
    variance = lax.optimization_barrier(jnp.mean(centered * centered, -1, keepdims=True))
    return centered * lax.rsqrt(variance + 1e-05)

def attend_block(query_rows, keys_all, values_all, seg_query, seg_keys):
    scale_factor = query_rows.shape[-1] ** (-0.5)
    scores = low_back(jnp.einsum('qhd,khd->hqk', query_rows, keys_all, precision=highest) * scale_factor)
    allowed = (seg_query[:, None] == seg_keys[None, :])[None]
    scores = jnp.where(allowed, scores, -1e+30)
    largest = lax.optimization_barrier(jnp.max(scores, -1, keepdims=True))
    weights = jnp.where(allowed, jnp.exp(scores - largest), 0.0)
    prob_rows = weights / lax.optimization_barrier(jnp.sum(weights, -1, keepdims=True))
    return jnp.einsum('hqk,khd->qhd', low(prob_rows), values_all, precision=highest)

def attention(query_all, keys_all, values_all, segments):
    length = query_all.shape[0]
    block_rows = math.gcd(length, 1024)
    count_blocks = length // block_rows
    blocked = query_all.reshape(count_blocks, block_rows, HEADS, HDIM)
    seg_blocks = segments.reshape(count_blocks, block_rows)

    def one_block(item_pair):
        return attend_block(item_pair[0], keys_all, values_all, item_pair[1], segments)
    result = lax.map(jax.checkpoint(one_block), (blocked, seg_blocks))
    return result.reshape(length, HEADS * HDIM)

def layer(seq_row, gain_attn, w_qkv, w_out, gain_ffn, w_up, w_down, segments):
    feature_count = seq_row.shape[-1]
    length = seq_row.shape[0]
    normed = low(normalize(seq_row) * gain_attn)
    projected = low_back(low(jnp.dot(normed, w_qkv, precision=highest)))
    query_all = projected[:, :feature_count].reshape(length, HEADS, HDIM)
    keys_all = projected[:, feature_count:2 * feature_count].reshape(length, HEADS, HDIM)
    values_all = projected[:, 2 * feature_count:].reshape(length, HEADS, HDIM)
    mixed = low_back(low(attention(query_all, keys_all, values_all, segments)))
    branch = low_back(jnp.dot(mixed, w_out, precision=highest))
    middle = seq_row + branch
    normed_two = low(normalize(middle) * gain_ffn)
    hidden = low_back(jnp.dot(normed_two, w_up, precision=highest))
    active = low(jax.nn.gelu(hidden, approximate=False))
    return middle + low_back(jnp.dot(active, w_down, precision=highest))

def reference(tokens, segment_ids, gain_attn, w_qkv, w_out, gain_ffn, w_up, w_down, cotangent):
    params = (gain_attn.astype(jnp.float32), w_qkv.astype(jnp.float32), w_out.astype(jnp.float32), gain_ffn.astype(jnp.float32), w_up.astype(jnp.float32), w_down.astype(jnp.float32))

    def one_sequence(accums, seq_item):
        seq_row, segments, upstream = seq_item

        def forward(start_row, *weight_list):
            return layer(start_row, *weight_list, segments)
        output, pullback = jax.vjp(forward, seq_row.astype(jnp.float32), *params)
        gradients = pullback(upstream.astype(jnp.float32))
        accums = tuple((accum + grad_one for accum, grad_one in zip(accums, gradients[1:])))
        return (accums, (output, gradients[0]))
    zeros_init = tuple((jnp.zeros_like(parameter) for parameter in params))
    accums, (outputs, input_grads) = lax.scan(one_sequence, zeros_init, (tokens, segment_ids, cotangent))
    return (outputs, input_grads, accums[0], accums[1], accums[2], accums[3], accums[4], accums[5])
```

```python
from functools import partial
import math
from types import SimpleNamespace

import jax
import jax.numpy as jnp
from jax import lax
from jax.experimental import pallas as pl
from jax.experimental.pallas import tpu as pltpu
from jax.sharding import PartitionSpec as P

HEADS = 12
NEG = -1e30
LOG2E = math.log2(math.e)
IMAGES = (197, 577)
REACH = 576
TILE = 128
UNIT = 128
F32, BF16 = jnp.float32, jnp.bfloat16
MESH = pl.DeviceIdType.MESH
NN = (((1,), (0,)), ((), ()))
NT = (((1,), (1,)), ((), ()))
BITS = ("core", "x", "z0", "z1", "y")
ORDER_A = ("core", "x", "y", "z0", "z1")
ORDER_B = ("core", "z0", "z1", "x", "y")
ORDER_C = ("core", "y", "x", "z0", "z1")
ORDER_D = ("core", "z0", "z1", "y", "x")
ORDER_E = ("core", "x", "z0", "z1", "y")
OUT_AFTER = 5
ORDERS = (ORDER_C, ORDER_E, ORDER_C, ORDER_E, ORDER_C, ORDER_E, ORDER_A, ORDER_E, ORDER_D, ORDER_C, ORDER_C, ORDER_D, ORDER_A, ORDER_D, ORDER_A, ORDER_D, ORDER_A)
ENDS = {
    ("ff", 2): ((0, 0), (1, 0),),
    ("ff", 4): ((0, 1), (2, 0), (3, 0),),
    ("dn", 1): ((2, 1),),
    ("dn", 2): ((3, 1), (4, 0), (5, 0),),
    ("gm", 0): ((0, 2), (1, 1),),
    ("de", 0): ((2, 2),),
    ("own", 0): ((0, 3), (2, 3), (1, 2), (3, 2), (4, 1), (5, 1), (6, 0),),
    ("own", 1): ((8, 0),),
    ("own", 2): ((0, 4), (2, 4), (1, 3), (3, 3), (4, 2), (5, 2), (7, 0),),
    ("own", 3): ((1, 4), (3, 4), (4, 3), (5, 3), (6, 1),),
    ("own", 4): ((4, 4), (5, 4), (8, 1),),
    ("out", 0): ((7, 1),),
    ("own", 5): ((6, 2), (9, 0),),
    ("oth", 2): ((7, 2), (8, 2),),
    ("oth", 3): ((6, 3), (9, 1),),
    ("oth", 4): ((8, 3), (10, 0), (11, 0), (12, 0),),
    ("oth", 5): ((6, 4), (7, 3), (9, 2), (13, 0), (14, 0),),
    ("tail", 0): ((8, 4), (11, 1), (12, 1), (15, 0), (16, 0),),
    ("tail", 1): ((7, 4), (9, 3), (14, 1),),
    ("tail", 2): ((13, 1),),
    ("tail", 4): ((12, 2), (10, 1),),
    ("tail", 5): ((16, 1),),
    ("tail", 6): ((11, 2),),
    ("tail", 7): ((14, 2), (9, 4), (11, 3), (12, 3), (16, 2), (15, 1), (14, 3), (10, 2), (13, 2), (11, 4), (12, 4), (16, 3), (13, 3), (14, 4), (13, 4), (16, 4), (15, 2), (10, 3), (15, 3), (10, 4), (15, 4),),
}


def dot(a, b, dims=NN):
    return lax.dot_general(a, b, dims, preferred_element_type=F32)


def aligned(value, unit):
    return pl.multiple_of(value, unit)


def tile_at(index):
    return pl.ds(aligned(index * TILE, TILE), TILE)


def chunks(total, size):
    return [(at, min(size, total - at)) for at in range(0, total, size)]


def interleave(first, second):
    first, second = list(first), list(second)
    done = 0
    for k, step in enumerate(first):
        step()
        upto = (k + 1) * len(second) // len(first)
        for other in second[done:upto]:
            other()
        done = upto
    for other in second[done:]:
        other()


def pipeline(before, during, after):
    count = len(during)
    for step in before[0]:
        step()
    for n in range(count):
        matrix = (list(after[n - 1]) if n else []) + (list(before[n + 1]) if n + 1 < count else [])
        interleave(matrix, during[n])
    for step in after[count - 1]:
        step()


def pair_rows(slab):
    first = lax.broadcasted_iota(jnp.int32, slab.shape, 1) < slab.shape[1] // 2
    zero = jnp.zeros_like(slab)
    return jnp.concatenate([jnp.where(first, slab, zero), jnp.where(first, zero, slab)], 0)


def own_halves(block):
    half = TILE // 2
    return jnp.concatenate([block[:half, :TILE], block[half:TILE, TILE:]], 0)


def fold_sum(block):
    return jnp.sum(block.reshape(block.shape[0] // 8, 8, block.shape[1]), 0)


def standardize(values):
    mean = jnp.mean(values, -1, keepdims=True)
    centered = values - mean
    variance = jnp.mean(centered * centered, -1, keepdims=True)
    inverse = lax.rsqrt(variance + 1e-05)
    return centered * inverse, inverse


def norm_backward(grad, normed, inverse):
    first = jnp.mean(grad, -1, keepdims=True)
    second = jnp.mean(grad * normed, -1, keepdims=True)
    return inverse * (grad - first - normed * second)


def near_keys(rows, t):
    return max(0, min(rows, REACH) - TILE * t)


def by_row_tiles(rows, body):
    def tile(i, _):
        for part in range(0, TILE, 32):
            body(pl.ds(aligned(i * TILE + part, 32), 32))
        return 0

    lax.fori_loop(0, rows // TILE, tile, 0)


def border_rows(rows):
    starts, found = {0}, {0}
    while found:
        found = {at + size for at in found for size in IMAGES if at + size < rows} - starts
        starts |= found
    reach = max(max(rows - at, at + size - rows) for at in starts for size in IMAGES if at < rows < at + size)
    return min(rows, -(-reach // 16) * 16)


def mark_segments(seg_ref, keys_ref, queries_ref, rows):
    for at, size in chunks(rows, TILE):
        column = jnp.broadcast_to(seg_ref[0:1, at : at + size].astype(F32), (TILE, size)).T
        same = column == lax.broadcasted_iota(jnp.int32, (size, TILE), 1).astype(F32)
        keys_ref[at : at + size, :] = jnp.where(same, 1.0, 0.0).astype(BF16)
        queries_ref[at : at + size, :] = jnp.where(same, 0.0, NEG).astype(BF16)


def both_rows(block):
    return jnp.concatenate([block, block], 0)


def with_marks(slab, marks):
    return jnp.concatenate([slab, marks], 1)


def shared_steps(sizes, most):
    groups = []
    for t, size in sorted(enumerate(sizes), key=lambda item: -item[1]):
        if not size:
            continue
        for group in groups:
            if sum(sizes[other] for other in group) + size <= most:
                group.append(t)
                break
        else:
            groups.append([t])
    return groups


def row_of(gain_ref):
    return jnp.concatenate([gain_ref[i : i + 1, :] for i in range(gain_ref.shape[0])], 1)


def norm_rows(x_ref, gain_ref, out_ref, rows, row_from=0):
    def tile(i, _):
        for part in range(0, 64, 32):
            at = pl.ds(aligned(row_from + i * 64 + part, 32), 32)
            normed, _ = standardize(x_ref[at, :].astype(F32))
            out_ref[at, :] = (normed * row_of(gain_ref)).astype(BF16)
        return 0

    lax.fori_loop(0, rows // 64, tile, 0)


def transpose_steps(src, base, into, row_from, count, width):
    def one(c, at, part):
        def step():
            rows_here = pl.ds(row_from + at if isinstance(row_from, int) else aligned(row_from + at, 64), part)
            into[c : c + TILE, at : at + part] = src[rows_here, base + c : base + c + TILE].T

        return step

    return [one(c, at, part) for c in range(0, width, TILE) for at, part in chunks(count, TILE)]


def project(a_ref, w_ref, out_ref, width, at, after_values):
    def one(c):
        def step():
            scale = 0.125 * LOG2E if c < width else 1.0
            out_ref[at, c : c + 256] = (dot(a_ref[at, :], w_ref[:, c : c + 256]) * scale).astype(BF16)

        return step

    for c in range(2 * width, 3 * width, 256):
        one(c)()
    interleave([one(c) for c in range(0, 2 * width, 256)], after_values)


def own_tile(t, tiles, me):
    return (tiles - 1 - t) * (1 - me) + t * me


def softmax_steps(items, scores_ref, probs_ref):
    count = len(items)

    def here(n, block, at, size):
        return slice(block["off"] + at, block["off"] + at + size), slice((n % 2) * 256, (n % 2) * 256 + 256)

    def scores(n):
        def one(block):
            def step():
                scores_ref[block["lane"]][here(n, block, 0, block["size"])] = dot(block["k"](), block["q2"](), NT)

            return step

        return [one(block) for block in items[n]]

    def largest(n):
        steps = []
        for block in items[n]:

            def part(at, block=block):
                def step():
                    new = scores_ref[block["lane"]][here(n, block, at, 32)]
                    block["max"] = jnp.maximum(block["max"], new) if at else new

                return step

            def last(block=block):
                top = jnp.max(block["max"], 0, keepdims=True)
                was = block["top"]()
                block["max"] = top if was is None else jnp.maximum(top, was)

            steps += [part(at) for at in range(0, block["size"], 32)] + [last]
        return steps

    def exponentials(n):
        def part(block, at, size):
            def step():
                s = scores_ref[block["lane"]][here(n, block, at, size)]
                probs_ref[block["lane"]][here(n, block, at, size)] = jnp.exp2(s - block["max"]).astype(BF16)

            return step

        return [part(block, at, size) for block in items[n] for at, size in chunks(block["size"], 64)]

    def values(n):
        def one(block):
            def step():
                vt = jnp.concatenate([block["vt"](), jnp.ones((16, block["size"]), BF16)], 0)
                mix = dot(vt, probs_ref[block["lane"]][here(n, block, 0, block["size"])])
                block["end"](block["max"], mix[TILE : TILE + 1, :], own_halves(mix))

            return step

        return [one(block) for block in items[n]]

    for step in scores(0) + largest(0):
        step()
    for n in range(count):
        interleave(scores(n + 1) if n + 1 < count else [], exponentials(n))
        interleave(values(n), largest(n + 1) if n + 1 < count else [])


def attend_local(r, rows, width):
    tiles, half_pairs = rows // TILE, width // TILE // 2

    def two_pairs(first, _):
        def one(k, u):
            hp = first + k * half_pairs
            lane = lambda base: pl.ds(aligned(base + hp * TILE, TILE), TILE)
            row_u = slice(u * TILE, u * TILE + TILE)

            def end(top, total, mix):
                r.top[pl.ds(hp * tiles + u, 1), :] = top
                r.total[pl.ds(hp * tiles + u, 1), :] = total
                r.gf[row_u, lane(0)] = mix

            return dict(
                size=rows, off=0, lane=k, top=lambda: None, end=end,
                q2=lambda: with_marks(pair_rows(r.pv[row_u, lane(0)]), both_rows(r.seg_q[row_u, :])),
                k=lambda: with_marks(r.pv[:, lane(width)], r.seg_k[...]),
                vt=lambda: r.act_t[lane(0), :rows],
            )

        softmax_steps([[one(k, u) for k in range(2)] for u in range(tiles)], (r.h, r.ga), (r.act, r.gh))
        return 0

    lax.fori_loop(0, half_pairs, two_pairs, 0)


def attend_cross(r, me, rows, width):
    tiles, half_pairs = rows // TILE, width // TILE // 2
    sizes = [near_keys(rows, t) for t in range(tiles)]

    def two_pairs(first, _):
        def one(k, t, off):
            hp = first + k * half_pairs
            lane = lambda base: pl.ds(aligned(base + hp * TILE, TILE), TILE)
            size = sizes[t]
            u = own_tile(t, tiles, me)
            i = hp * tiles + u
            keys = pl.ds(aligned((rows - size) * me, 64), size)
            lanes = pl.ds(aligned(TILE * t * me, TILE), size)

            def end(top, total, mix):
                top_was, total_was = r.top[pl.ds(i, 1), :], r.total[pl.ds(i, 1), :]
                fade = jnp.exp2(top_was - top)
                total = total_was * fade + total
                over = 1.0 / total
                half = TILE // 2
                by_head = lambda row: jnp.concatenate(
                    [jnp.broadcast_to(row[:, :TILE], (half, TILE)), jnp.broadcast_to(row[:, TILE:], (half, TILE))], 0
                )
                done = (r.gf[tile_at(u), lane(0)] * by_head(fade) + mix) * by_head(over)
                r.mixedv[tile_at(u), lane(0)] = done.T.astype(BF16)
                r.stats[0, pl.ds(hp * tiles + t, 1), :] = top + jnp.log2(total)

            return dict(
                size=size, off=off, lane=k, top=lambda: r.top[pl.ds(i, 1), :], end=end,
                q2=lambda: with_marks(pair_rows(r.pv[tile_at(u), lane(0)]), both_rows(r.seg_q[tile_at(u), :])),
                k=lambda: with_marks(r.prv[keys, lane(width)], r.seg_kr[keys, :]),
                vt=lambda: r.act_t[pl.ds(aligned(width + hp * TILE, TILE), TILE), lanes],
            )

        items = []
        for group in shared_steps(sizes, rows):
            offs = [sum(sizes[other] for other in group[:n]) for n in range(len(group))]
            items.append([one(k, t, off) for t, off in zip(group, offs) for k in range(2)])
        softmax_steps(items, (r.h, r.ga), (r.act, r.gh))

        for t in range(tiles):
            if not sizes[t]:
                for k in range(2):
                    no_neighbour(first + k * half_pairs, t)
        return 0

    def no_neighbour(hp, t):
        lane = pl.ds(aligned(hp * TILE, TILE), TILE)
        u = own_tile(t, tiles, me)
        i = hp * tiles + u
        total = r.total[pl.ds(i, 1), :]
        over = 1.0 / total
        half = TILE // 2
        scale = jnp.concatenate(
            [jnp.broadcast_to(over[:, :TILE], (half, TILE)), jnp.broadcast_to(over[:, TILE:], (half, TILE))], 0
        )
        r.mixedv[tile_at(u), lane] = (r.gf[tile_at(u), lane] * scale).T.astype(BF16)
        r.stats[0, pl.ds(hp * tiles + t, 1), :] = r.top[pl.ds(i, 1), :] + jnp.log2(total)

    lax.fori_loop(0, half_pairs, two_pairs, 0)


INV_SQRT2PI = 1.0 / math.sqrt(2.0 * math.pi)
TAIL_SLOPE = 0.3275911 * math.sqrt(0.5)
TAIL = tuple(0.5 * c for c in (0.254829592, -0.284496736, 1.421413741, -1.453152027, 1.061405429))


def gelu_parts(h):
    below_one = 1.0 + TAIL_SLOPE * jnp.abs(h)
    t = pl.reciprocal(below_one, approx=True)
    t = t * (2.0 - below_one * t)
    bell = jnp.exp2(h * h * (-0.5 * LOG2E))
    poly = TAIL[4]
    for c in TAIL[3::-1]:
        poly = poly * t + c
    tail = poly * t * bell
    below = jnp.where(h < 0.0, tail, 1.0 - tail)
    return below, below + h * bell * INV_SQRT2PI


def where_am_i():
    dp, blk = lax.axis_index("dp"), lax.axis_index("blk")
    bits = {name: lax.rem(lax.div(dp, 2**k), 2) for k, name in enumerate(BITS[:-1])}
    bits["y"] = blk
    return dp, blk, bits


def partner_of(name, dp, blk, bits):
    if name == "y":
        return {"blk": 1 - blk}
    return {"dp": dp + 2 ** BITS.index(name) * (1 - 2 * bits[name])}


def block_index(order, d, y):
    bits = {name: (d >> k) & 1 for k, name in enumerate(BITS[:-1])}
    bits["y"] = y
    index = 0
    for name in order:
        index = 2 * index + bits[name]
    return index


class Reducer:
    def __init__(self, r):
        self.r = r
        self.dp, self.blk, self.bits = where_am_i()

    def keep(self, order, stage):
        base = 0
        for k in range(stage + 1):
            base = base + self.bits[order[k]] * (16 >> k)
        return base

    def copy(self, chunk, stage):
        number, unit, units, order, _ = chunk
        half = 16 >> stage
        base = self.keep(order, stage - 1) if stage else 0
        away = base + (1 - self.bits[order[stage]]) * half
        slot = 32 - 2 * half
        return pltpu.make_async_remote_copy(
            src_ref=self.r.g.at[pl.ds(unit, units), pl.ds(away, half)],
            dst_ref=self.r.recv.at[pl.ds(unit, units), pl.ds(slot, half)],
            send_sem=self.r.rs_sent.at[number, stage],
            recv_sem=self.r.rs_got.at[number, stage],
            device_id=partner_of(order[stage], self.dp, self.blk, self.bits),
            device_id_type=MESH,
        )

    def start(self, chunk, stage=0):
        self.copy(chunk, stage).start()

    def finish(self, chunk, stage):
        number, unit, units, order, write = chunk
        half = 16 >> stage
        self.copy(chunk, stage).wait()
        keep = self.keep(order, stage)
        slot = 32 - 2 * half
        if stage == 4:
            for k in range(units):
                write(k, self.r.g[unit + k, keep].astype(F32) + self.r.recv[unit + k, slot].astype(F32))
            return
        step = min(half, 4)

        def add(j, _):
            for k in range(units):
                mine = pl.ds(keep + j * step, step)
                self.r.g[unit + k, mine] += self.r.recv[unit + k, pl.ds(slot + j * step, step)]
            return 0

        if half == step:
            add(0, 0)
        else:
            lax.fori_loop(0, half // step, add, 0)
        self.start(chunk, stage + 1)


def kernel_layer(names, *refs):
    r = SimpleNamespace(**dict(zip(names, refs)))
    rows, width = r.xv.shape
    ff = r.wb.shape[0]
    me = lax.axis_index("blk")
    reach, tiles, pairs = min(rows, REACH), rows // TILE, width // TILE
    red = Reducer(r)
    dp, blk, bits = red.dp, red.blk, red.bits

    barrier = pltpu.get_barrier_semaphore()
    for name in BITS:
        pl.semaphore_signal(
            barrier, inc=1, device_id=partner_of(name, dp, blk, bits), device_id_type=MESH
        )
    loads = {}
    for k, (src, into) in enumerate(
        [("x", r.xv), ("w_qkv", r.wa.at[:, : 3 * width]), ("w_out", r.wo), ("cot", r.cotv), ("w_down", r.wb)]
    ):
        loads[src] = pltpu.make_async_copy(getattr(r, src), into, r.loads.at[k])
        loads[src].start()
    loads["w_up"] = pltpu.make_async_copy(r.w_up, r.wa, r.loads.at[5])
    load_w_qkv = pltpu.make_async_copy(r.w_qkv, r.wa.at[:, : 3 * width], r.loads.at[6])
    near, span = rows // 2, border_rows(rows)
    far = pl.ds(aligned(span * (1 - me), 16), rows - span)
    give = pl.ds(aligned((rows - span) * (1 - me), 16), span)
    give_near = pl.ds(aligned((rows - near) * (1 - me), 16), near)
    give_far = pl.ds(aligned((rows - span) * (1 - me) + near * me, 16), span - near)
    to_y = dict(device_id={"blk": 1 - me}, device_id_type=MESH)
    if span < rows:
        r.xr[far, :] = jnp.zeros((rows - span, width), BF16)
        r.gmr[far, :] = jnp.zeros((rows - span, width), BF16)
    loads["x"].wait()
    pl.semaphore_wait(barrier, len(BITS))

    def to_neighbour(k, src, dst):
        copy = pltpu.make_async_remote_copy(
            src_ref=src, dst_ref=dst, send_sem=r.sent.at[k], recv_sem=r.got.at[k], **to_y
        )
        copy.start()
        return copy

    send_near = to_neighbour(0, r.xv.at[give_near], r.xr.at[give_near])
    send_seg = to_neighbour(1, r.seg, r.segr)
    send_far = to_neighbour(4, r.xv.at[give_far], r.xr.at[give_far])
    norm_rows(r.xv, r.gain_attn, r.ffn_in, rows)
    mark_segments(r.seg, r.seg_k, r.seg_q, rows)
    loads["w_qkv"].wait()
    project(r.ffn_in, r.wa, r.pv, width, slice(None), transpose_steps(r.pv, 2 * width, r.act_t, 0, rows, width))
    attend_local(r, rows, width)

    send_seg.wait()
    mark_segments(r.segr, r.seg_kr, r.seg_qr, rows)

    def neighbour_half(n, _):
        pl.when(n == 0)(send_near.wait)
        pl.when(n == 1)(send_far.wait)
        row_from = near * (me * (1 - n) + (1 - me) * n)
        norm_rows(r.xr, r.gain_attn, r.ffn_in, near, row_from)
        project(r.ffn_in, r.wa, r.prv, width, pl.ds(aligned(row_from, 64), near), [])
        return 0

    lax.fori_loop(0, 2, neighbour_half, 0)
    loads["w_up"].start()
    for step in transpose_steps(r.prv, 2 * width, r.act_t.at[width : 2 * width, :], (rows - reach) * me, reach, width):
        step()
    attend_cross(r, me, rows, width)

    block_rows = width // 16

    def put(unit, order, d, y, row, block):
        r.g[unit, block_index(order, d, y), row : row + block.shape[0], :] = block

    def into(ref, base):
        def write(k, block):
            ref[:, tile_at(base + k)] = block

        return write


    def up_unit(i, k):
        return lax.div(i, 2) * 4 + 2 * k + lax.rem(i, 2) if not isinstance(i, int) else i // 2 * 4 + 2 * k + i % 2

    def chunk_up(c, k):
        def write(m, block):
            r.o_up[:, tile_at(4 * c + 2 * m + k)] = block

        return (2 * c + k, 4 * c + 2 * k, 2, ORDERS[k], write)

    def chunk_down(j):
        def write(k, block):
            r.o_down[k * block_rows : (k + 1) * block_rows, j * UNIT : (j + 1) * UNIT] = block

        return (6 + j, 12 + 4 * j, 4, ORDERS[6 + j], write)

    out_chunk = (9, 0, 3, ORDERS[9], into(r.o_out, 0))

    middle_chunk = (10, 6, 3, ORDERS[10], into(r.o_qkv, 3))

    def chunk_qkv(n, k):
        j = n + 6 * k
        return (11 + 2 * n + k, 3 + j, 1, ORDERS[11 + k], into(r.o_qkv, j))

    table = [chunk_up(c, k) for c in range(3) for k in range(2)] + [chunk_down(j) for j in range(3)]
    table += [out_chunk, middle_chunk] + [chunk_qkv(n, k) for n in range(3) for k in range(2)]

    def ends(name, step):
        for chunk, stage in ENDS.get((name, step), ()):
            red.finish(table[chunk], stage)

    def ends_in_loop(name, index, steps):
        for step in steps:
            if (name, step) in ENDS:
                pl.when(index == step)(lambda step=step: ends(name, step))

    loads["w_out"].wait()
    for c, part in chunks(width, 256):
        r.mid[:, c : c + part] = r.xv[:, c : c + part].astype(F32) + dot(r.mixedv[...], r.wo[:, c : c + part])

    def norm_two(at):
        normed, _ = standardize(r.mid[at, :])
        r.ffn_in[at, :] = (normed * row_of(r.gain_ffn)).astype(BF16)
        r.lo[at, :] = r.mid[at, :]
        r.gf[at, :] = jnp.zeros_like(r.gf[at, :])

    norm_two_steps = [lambda at=at: norm_two(slice(at, at + 32)) for at in range(0, rows, 32)]
    norm_two_steps += transpose_steps(r.ffn_in, 0, r.ffn_t, 0, rows, width)
    for src in ("w_up", "cot", "w_down"):
        loads[src].wait()

    def column(n, i):
        return pl.ds(aligned((n % 2) * (ff // 2) + i * 256, 256), 256)

    def side(n):
        return slice((n % 2) * 256, (n % 2) * 256 + 256)

    def ff_before(n, i):
        def up():
            r.h[:, side(n)] = dot(r.ffn_in[...], r.wa[:, column(n, i)])

        def down():
            r.ga[:, side(n)] = dot(r.cotv[...], r.wb[column(n, i), :], NT)

        return [up, down]

    def ff_during(n):
        def part(row):
            def step():
                tile = slice(row, row + 32)
                h = r.h[tile, side(n)]
                below, slope = gelu_parts(h)
                r.act[tile, side(n)] = (h * below).astype(BF16)
                r.gh[tile, side(n)] = (slope * r.ga[tile, side(n)]).astype(BF16)

            return step

        return [part(row) for row in range(0, rows, 32)]

    def ff_after(n, i):
        def out(c):
            def step():
                r.lo[:, c : c + 256] += dot(r.act[:, side(n)], r.wb[column(n, i), c : c + 256])

            return step

        def back(c):
            def step():
                r.gf[:, c : c + 256] += dot(r.gh[:, side(n)], r.wa[c : c + 256, column(n, i)], NT)

            return step

        def weights():
            grad = dot(r.ffn_t[...], r.gh[:, side(n)]).astype(BF16)
            for d in range(16):
                for k in range(2):
                    put(up_unit(i, k), ORDERS[k], d, n % 2, 0,
                        grad[d * block_rows : (d + 1) * block_rows, k * UNIT : (k + 1) * UNIT])

        def turn():
            base = (n % 2) * (ff // 2) + i * 256
            for c in range(0, 256, TILE):
                for row in range(0, rows, TILE):
                    r.act_t[pl.ds(aligned(base + c, TILE), TILE), row : row + TILE] = r.act[
                        row : row + TILE, (n % 2) * 256 + c : (n % 2) * 256 + c + TILE].T

        return [weights] + [step(c) for step in (out, back) for c in range(0, width, 256)] + [turn]

    last = ff // 512 - 1
    interleave([ff_before(0, 0)[1], ff_before(1, 0)[1]], norm_two_steps)
    ff_before(0, 0)[0]()
    interleave(ff_before(1, 0)[:1], ff_during(0))

    def ff_two(i, _):
        interleave(ff_after(0, i) + ff_before(0, i + 1), ff_during(1))
        interleave(ff_after(1, i) + ff_before(1, i + 1), ff_during(0))

        @pl.when(lax.rem(i, 2) == 1)
        def _():
            for k in range(2):
                red.start(chunk_up(lax.div(i, 2), k))

        ends_in_loop("ff", i, range(last))
        return 0

    lax.fori_loop(0, last, ff_two, 0)
    interleave(ff_after(0, last), ff_during(1))
    for step in ff_after(1, last):
        step()
    for k in range(2):
        red.start(chunk_up(last // 2, k))
    ends("ff", last)
    load_w_qkv.start()
    out_lo = pltpu.make_async_copy(r.lo, r.layer_out, r.loads.at[7])
    out_lo.start()

    def grad_down(j):
        order = ORDERS[6 + j]

        def part(c):
            def step():
                both = jnp.concatenate(
                    [r.cotv[:, half * (width // 2) + j * UNIT : half * (width // 2) + (j + 1) * UNIT]
                     for half in range(2)], 1)
                grad = dot(r.act_t[c : c + width, :], both).astype(BF16)
                for part in range(4):
                    for k in range(4):
                        for half in range(2):
                            at = part * 4 * block_rows + k * block_rows
                            put(12 + 4 * j + k, order, 4 * (c // width) + part, half, 0,
                                grad[at : at + block_rows, half * UNIT : (half + 1) * UNIT])

            return step

        return [part(c) for c in range(0, ff, width)]

    r.gains[...] = jnp.zeros_like(r.gains)

    def norm_two_back(at):
        def step():
            normed, inverse = standardize(r.mid[at, :])
            grad = r.gf[at, :]
            r.gains[0:8, :] += fold_sum(grad * normed)
            grad = r.cotv[at, :].astype(F32) + norm_backward(
                grad * row_of(r.gain_ffn), normed, inverse
            )
            r.gf[at, :] = grad
            r.ffn_in[at, :] = grad.astype(BF16)

        return step

    def norm_one_again(at):
        def step():
            normed, _ = standardize(r.xv[at, :].astype(F32))
            r.xr[at, :] = (normed * row_of(r.gain_attn)).astype(BF16)

        return step

    row_tiles = [slice(at, at + 32) for at in range(0, rows, 32)]
    beside = [
        [norm_two_back(at) for at in row_tiles],
        [norm_one_again(at) for at in row_tiles] + transpose_steps(r.mixedv, 0, r.ffn_t, 0, rows, width),
        transpose_steps(r.xr, 0, r.n1_t, 0, rows, width) + transpose_steps(r.pv, width, r.kt, 0, rows, width)
        + transpose_steps(r.prv, width, r.ktr, (rows - reach) * me, reach, width),
    ]
    for j in range(3):
        for n, step in enumerate(grad_down(j)):
            share = beside[j][n * len(beside[j]) // 4 : (n + 1) * len(beside[j]) // 4]
            pl.when(me >= 0)(lambda step=step, share=share: interleave([step], share))
        red.start(chunk_down(j))
        ends("dn", j)

    for c, part in chunks(width, 256):
        r.gm[:, c : c + part] = dot(r.ffn_in[...], r.wo[c : c + part, :], NT).astype(BF16)
    send_gm = to_neighbour(2, r.gm.at[give], r.gmr.at[give])
    ends("gm", 0)

    def delta_rows(hp, _):
        lane = tile_at(hp)
        half = TILE // 2
        for t in range(tiles):
            at = tile_at(own_tile(t, tiles, me))
            both = (r.gm[at, lane].astype(F32) * r.mixedv[at, lane].astype(F32)).T
            first = jnp.sum(both[:half, :], 0, keepdims=True)
            second = jnp.sum(both[half:, :], 0, keepdims=True)
            r.stats[1, pl.ds(hp * tiles + t, 1), :] = jnp.concatenate([first, second], 1)
        return 0

    lax.fori_loop(0, pairs, delta_rows, 0)
    send_stats = to_neighbour(3, r.stats, r.statsr)
    ends("de", 0)

    out_lo.wait()

    def grad_steps(items):
        def here(n, block, at, size):
            return slice(block["off"] + at, block["off"] + at + size), side(n)

        def before(n):
            def scores(block):
                def step():
                    r.h[here(n, block, 0, block["size"])] = dot(block["k"](), block["q2"](), NT)

                return step

            def probs(block):
                def step():
                    r.ga[here(n, block, 0, block["size"])] = dot(block["v"](), block["do2"](), NT)

                return step

            return [step(block) for block in items[n] for step in (scores, probs)]

        def during(n):
            def part(block, at, size):
                def step():
                    rows_here = here(n, block, at, size)
                    p = jnp.exp2(r.h[rows_here] - block["lse"]())
                    r.act[rows_here] = p.astype(BF16)
                    r.gh[rows_here] = (p * (r.ga[rows_here] - block["delta"]())).astype(BF16)

                return step

            return [part(block, at, size) for block in items[n] for at, size in chunks(block["size"], 64)]

        def after(n):
            steps = []
            for block in items[n]:
                rows_here = here(n, block, 0, block["size"])
                steps += block["after"](lambda at=rows_here: r.act[at], lambda at=rows_here: r.gh[at])
            return steps

        count = range(len(items))
        pipeline([before(n) for n in count], [during(n) for n in count], [after(n) for n in count])

    sizes = [near_keys(rows, t) for t in range(tiles)]
    groups = shared_steps(sizes, rows)

    def offsets(group):
        return [(t, sum(sizes[other] for other in group[:n])) for n, t in enumerate(group)]

    def own_queries(hp):
        lane = lambda base: pl.ds(aligned(base + hp * TILE, TILE), TILE)
        parts = [[] for _ in range(tiles)]

        def base(t):
            at_u = tile_at(own_tile(t, tiles, me))
            return dict(
                q2=lambda: with_marks(pair_rows(r.pv[at_u, lane(0)]), both_rows(r.seg_q[at_u, :])),
                do2=lambda: pair_rows(r.gm[at_u, lane(0)]),
                lse=lambda: r.stats[0, pl.ds(hp * tiles + t, 1), :],
                delta=lambda: r.stats[1, pl.ds(hp * tiles + t, 1), :],
            )

        def add_queries(t, new):
            parts[t].append(new)
            if len(parts[t]) == (2 if sizes[t] else 1):
                dq = own_halves(sum(parts[t][1:], parts[t][0])) * 0.125
                r.mixedv[tile_at(own_tile(t, tiles, me)), lane(0)] = dq.T.astype(BF16)

        def local(t):
            mine = base(t)

            def after(p, ds):
                def queries():
                    add_queries(t, dot(r.kt[lane(0), :], ds()))

                def values():
                    new = dot(p(), mine["do2"]())
                    r.mid[:, lane(0)] = new if t == 0 else r.mid[:, lane(0)] + new

                def keys():
                    new = dot(ds(), pair_rows(r.pv[tile_at(own_tile(t, tiles, me)), lane(0)]))
                    r.lo[:, lane(0)] = new if t == 0 else r.lo[:, lane(0)] + new

                return [queries, values, keys]

            return dict(mine, size=rows, off=0, after=after, v=lambda: r.pv[:, lane(2 * width)],
                        k=lambda: with_marks(r.pv[:, lane(width)], r.seg_k[...]))

        def cross(t, off):
            keys = pl.ds(aligned((rows - sizes[t]) * me, 64), sizes[t])
            lanes = pl.ds(aligned(TILE * t * me, TILE), sizes[t])

            def after(p, ds):
                def queries():
                    add_queries(t, dot(r.ktr[lane(0), lanes], ds()))

                return [queries]

            return dict(base(t), size=sizes[t], off=off, after=after, v=lambda: r.prv[keys, lane(2 * width)],
                        k=lambda: with_marks(r.prv[keys, lane(width)], r.seg_kr[keys, :]))

        items = []
        for t in range(tiles):
            items.append([local(t)])
            if t < len(groups):
                items.append([cross(other, off) for other, off in offsets(groups[t])])
        grad_steps(items)

    def other_queries(hp):
        lane = lambda base: pl.ds(aligned(base + hp * TILE, TILE), TILE)

        def block(t, off):
            at_u = tile_at(t * (1 - me) + (tiles - 1 - t) * me)
            keys = pl.ds(aligned((rows - sizes[t]) * (1 - me), 64), sizes[t])

            def after(p, ds):
                def values():
                    r.mid[keys, lane(0)] += dot(p(), pair_rows(r.gmr[at_u, lane(0)]))

                def scores():
                    r.lo[keys, lane(0)] += dot(ds(), pair_rows(r.prv[at_u, lane(0)]))

                return [values, scores]

            return dict(
                size=sizes[t], off=off, after=after,
                q2=lambda: with_marks(pair_rows(r.prv[at_u, lane(0)]), both_rows(r.seg_qr[at_u, :])),
                do2=lambda: pair_rows(r.gmr[at_u, lane(0)]),
                lse=lambda: r.statsr[0, pl.ds(hp * tiles + t, 1), :],
                delta=lambda: r.statsr[1, pl.ds(hp * tiles + t, 1), :],
                k=lambda: with_marks(r.pv[keys, lane(width)], r.seg_k[keys, :]),
                v=lambda: r.pv[keys, lane(2 * width)],
            )

        grad_steps([[block(t, off) for t, off in offsets(group)] for group in groups])
        r.pv[:, lane(width)] = (r.lo[:, lane(0)] * (1.0 / LOG2E)).astype(BF16)
        r.pv[:, lane(2 * width)] = r.mid[:, lane(0)].astype(BF16)

    def own_pass(hp, _):
        own_queries(hp)
        ends_in_loop("own", hp, range(pairs))
        return 0

    lax.fori_loop(0, OUT_AFTER, own_pass, 0)
    for n, name in enumerate(BITS):
        pl.semaphore_signal(
            r.again.at[n], inc=1, device_id=partner_of(name, dp, blk, bits), device_id_type=MESH
        )

    for c, part in chunks(width, 256):
        grad = dot(r.ffn_t[...], r.ffn_in[:, c : c + part]).astype(BF16)
        for k in range(2):
            column_at = c + k * UNIT
            y, unit = column_at // (width // 2), column_at % (width // 2) // UNIT
            for d in range(16):
                put(unit, ORDERS[9], d, y, 0,
                    grad[d * block_rows : (d + 1) * block_rows, k * UNIT : (k + 1) * UNIT])
    for k in range(len(BITS)):
        pl.semaphore_wait(r.again.at[k], 1)
    red.start(out_chunk)
    ends("out", 0)
    lax.fori_loop(OUT_AFTER, pairs, own_pass, 0)

    send_gm.wait()
    send_stats.wait()
    r.pv[:, :width] = r.mixedv[...]

    def grad_qkv(j, order):
        columns = [pl.ds(aligned(y * (3 * width // 2) + j * UNIT, UNIT), UNIT) for y in range(2)]
        grad = dot(r.n1_t[...], jnp.concatenate([r.pv[:, at] for at in columns], 1)).astype(BF16)
        for y in range(2):
            for d in range(16):
                put(3 + j, order, d, y, 0,
                    grad[d * block_rows : (d + 1) * block_rows, y * UNIT : (y + 1) * UNIT])

    half_pairs = pairs // 2

    def first_pass(hp, _):
        other_queries(hp)
        grad_qkv(half_pairs + hp, ORDERS[10])

        @pl.when(hp == half_pairs - 1)
        def _():
            red.start(middle_chunk)

        ends_in_loop("oth", hp, range(half_pairs))
        return 0

    lax.fori_loop(0, half_pairs, first_pass, 0)

    def second_pass(hp, _):
        other_queries(hp)
        for k in range(2):
            grad_qkv(hp - half_pairs + 6 * k, ORDERS[11 + k])
            red.start(chunk_qkv(hp - half_pairs, k))
        ends_in_loop("oth", hp, range(half_pairs, pairs))
        return 0

    lax.fori_loop(half_pairs, pairs, second_pass, 0)

    load_w_qkv.wait()
    for c, part in chunks(width, 256):
        r.lo[:, c : c + part] = dot(r.pv[...], r.wa[c : c + part, : 3 * width], NT)
    ends("tail", 0)

    def norm_one_back(at):
        normed, inverse = standardize(r.xv[at, :].astype(F32))
        grad = r.lo[at, :]
        r.gains[8:16, :] += fold_sum(grad * normed)
        r.mid[at, :] = r.gf[at, :] + norm_backward(
            grad * row_of(r.gain_attn), normed, inverse
        )

    by_row_tiles(rows, norm_one_back)
    ends("tail", 1)
    out_gin = pltpu.make_async_copy(r.mid, r.input_grad, r.loads.at[8])
    out_gin.start()
    r.o_gains[0] = jnp.concatenate(
        [jnp.sum(r.gains[0:8, :], 0, keepdims=True), jnp.sum(r.gains[8:16, :], 0, keepdims=True),
         jnp.zeros((6, width), F32)], 0)

    def gain_copy(k):
        return pltpu.make_async_remote_copy(
            src_ref=r.o_gains.at[k], dst_ref=r.gains_in.at[k], send_sem=r.gain_sent.at[k], recv_sem=r.gain_got.at[k],
            device_id=partner_of(ORDER_A[k], dp, blk, bits), device_id_type=MESH)

    gain_copy(0).start()
    for k in range(5):
        ends("tail", 2 + k)
        gain_copy(k).wait()
        r.o_gains[k + 1] = r.o_gains[k] + r.gains_in[k]
        if k + 1 < 5:
            gain_copy(k + 1).start()
    ends("tail", 7)
    out_gin.wait()


def call_layer(x, seg, gain_attn, gain_ffn, w_qkv, w_out, w_up, w_down, cot):
    rows, width = x.shape
    ff = w_down.shape[0]
    tiles, pairs, block = rows // TILE, width // TILE, width // 16
    stat = (-(-pairs * tiles // 8) * 8, 2 * TILE)
    vmem = pl.BlockSpec(memory_space=pltpu.VMEM)
    anywhere = pl.BlockSpec(memory_space=pl.ANY)
    ins = dict(x=anywhere, seg=vmem, gain_attn=vmem, gain_ffn=vmem, w_qkv=anywhere, w_out=anywhere,
               w_up=anywhere, w_down=anywhere, cot=anywhere)
    outs = dict(
        layer_out=((rows, width), F32, anywhere), input_grad=((rows, width), F32, anywhere),
        o_gains=((6, 8, width), F32, vmem), o_qkv=((block, 3 * width // 2), F32, vmem),
        o_out=((block, width // 2), F32, vmem), o_up=((block, ff // 2), F32, vmem),
        o_down=((ff // 16, width // 2), F32, vmem),
    )
    big = ((rows, width), BF16)
    wide = ((rows, width), F32)
    scratch = dict(
        xv=big, xr=big, mixedv=big, cotv=big, pv=((rows, 3 * width), BF16), prv=((rows, 3 * width), BF16),
        wo=((width, width), BF16), wa=((width, ff), BF16), wb=((ff, width), BF16),
        mid=wide, lo=wide, gf=wide, ffn_in=big, ffn_t=((width, rows), BF16), act_t=((ff, rows), BF16),
        h=((rows, 512), F32), ga=((rows, 512), F32), act=((rows, 512), BF16), gh=((rows, 512), BF16),
        gmr=big, stats=((2,) + stat, F32), statsr=((2,) + stat, F32), top=(stat, F32), total=(stat, F32),
        segr=((1, rows), jnp.int32), seg_k=((rows, TILE), BF16), seg_q=((rows, TILE), BF16),
        seg_kr=((rows, TILE), BF16), seg_qr=((rows, TILE), BF16),
        gains=((16, width), F32), gains_in=((5, 8, width), F32),
        g=((24, 32, block, UNIT), BF16), recv=((24, 31, block, UNIT), BF16),
    )
    sems = dict(loads=(9,), sent=(5,), got=(5,), rs_sent=(17, 5), rs_got=(17, 5), gain_sent=(5,), gain_got=(5,))
    names = list(ins) + list(outs) + list(scratch) + list(sems) + ["again"]

    def body(*refs):
        r = dict(zip(names, refs))
        wb = r["wb"]
        extra = dict(
            kt=wb.at[0:width, 0:rows], ktr=wb.at[width : 2 * width, 0:rows],
            n1_t=wb.at[2 * width : 3 * width, 0:rows], gm=wb.at[3 * width : 3 * width + rows, :],
        )
        kernel_layer(list(r) + list(extra), *r.values(), *extra.values())

    return pl.pallas_call(
        body,
        out_shape=[jax.ShapeDtypeStruct(v[0], v[1]) for v in outs.values()],
        in_specs=list(ins.values()),
        out_specs=[v[2] for v in outs.values()],
        scratch_shapes=[pltpu.VMEM(*v) for v in scratch.values()]
        + [pltpu.SemaphoreType.DMA(n) for n in sems.values()]
        + [pltpu.SemaphoreType.REGULAR((len(BITS),))],
        compiler_params=pltpu.CompilerParams(
            collective_id=0, has_side_effects=True, vmem_limit_bytes=60 * 2**20
        ),
        name="layer",
    )(x, seg, gain_attn, gain_ffn, w_qkv, w_out, w_up, w_down, cot)


def padded(block, sides, width):
    for axis, dim in sides:
        count = lax.axis_size(axis)
        forward = [(i, i + 1) for i in range(count - 1)]
        backward = [(target, source) for source, target in forward]
        low = lax.ppermute(
            lax.slice_in_dim(block, block.shape[dim] - width, None, axis=dim), axis, forward
        )
        high = lax.ppermute(lax.slice_in_dim(block, 0, width, axis=dim), axis, backward)
        block = jnp.concatenate([low, block, high], axis=dim)
    return block


def from_behind(block, axis, distance):
    devices = range(lax.axis_size(axis))
    route = [(i - distance, i) for i in devices if i - distance in devices]
    return lax.ppermute(block, axis, route)


def normalize(values):
    centered = values - jnp.mean(values, -1, keepdims=True)
    variance = jnp.mean(centered * centered, -1, keepdims=True)
    inverse = lax.rsqrt(variance + 1e-05)
    return (centered * inverse, inverse)


def norm_back(grad_normed, normed, inverse):
    first = jnp.mean(grad_normed, -1, keepdims=True)
    second = jnp.mean(grad_normed * normed, -1, keepdims=True)
    return inverse * (grad_normed - first - normed * second)


def split_blocks(packed, seg_all):
    length = packed.shape[0]
    feature_count = packed.shape[1] // 2
    block_rows = math.gcd(length, 512)
    count_blocks = length // block_rows
    keys_blk = packed[:, :feature_count].reshape(
        count_blocks, block_rows, HEADS, feature_count // HEADS
    )
    vals_blk = packed[:, feature_count:].reshape(
        count_blocks, block_rows, HEADS, feature_count // HEADS
    )
    seg_blk = seg_all.reshape(count_blocks, block_rows)
    return (keys_blk, vals_blk, seg_blk)


def fetch_near(kv_local, seg_mark):
    return (
        padded(kv_local, (("blk", 0),), kv_local.shape[0]),
        padded(seg_mark, (("blk", 0),), kv_local.shape[0]),
    )


def block_scores(query_rows, keys_rows, seg_query, seg_keys):
    scale_factor = query_rows.shape[-1] ** (-0.5)
    scores = (
        jnp.einsum("qhd,khd->hqk", query_rows, keys_rows, preferred_element_type=jnp.float32)
        * scale_factor
    )
    allowed = (seg_query[:, None] == seg_keys[None, :])[None]
    return (jnp.where(allowed, scores, -1e30), allowed)


def attend_forward(query_rows, keys_blk, vals_blk, seg_blk, seg_query):
    row_count = query_rows.shape[0]

    def stats_step(carried, block_item):
        running, totals = carried
        scores, allowed = block_scores(query_rows, block_item[0], seg_query, block_item[1])
        newest = jnp.maximum(running, jnp.max(scores, -1))
        fresh = jnp.sum(jnp.where(allowed, jnp.exp(scores - newest[..., None]), 0.0), -1)
        return ((newest, totals * jnp.exp(running - newest) + fresh), None)

    start_max = jnp.full((HEADS, row_count), -1e30, jnp.float32)
    start_tot = jnp.zeros((HEADS, row_count), jnp.float32)
    (running, totals), unused = lax.scan(stats_step, (start_max, start_tot), (keys_blk, seg_blk))
    logsum = running + jnp.log(totals)

    def value_step(carried, block_item):
        scores, allowed = block_scores(query_rows, block_item[0], seg_query, block_item[2])
        prob_rows = jnp.where(allowed, jnp.exp(scores - logsum[..., None]), 0.0).astype(
            jnp.bfloat16
        )
        return (
            carried
            + jnp.einsum(
                "hqk,khd->qhd", prob_rows, block_item[1], preferred_element_type=jnp.float32
            ),
            None,
        )

    start_mix = jnp.zeros(query_rows.shape, jnp.float32)
    mixed, unused_two = lax.scan(value_step, start_mix, (keys_blk, vals_blk, seg_blk))
    return (mixed, logsum)


def attend_backward(
    query_rows, keys_blk, vals_blk, seg_blk, seg_query, logsum, grad_mixed, delta_rows
):
    scale_factor = query_rows.shape[-1] ** (-0.5)

    def grad_step(carried, block_item):
        keys_rows, vals_rows, seg_keys = block_item
        scores, allowed = block_scores(query_rows, keys_rows, seg_query, seg_keys)
        prob_rows = jnp.where(allowed, jnp.exp(scores - logsum[..., None]), 0.0)
        grad_vals = jnp.einsum(
            "hqk,qhd->khd",
            prob_rows.astype(jnp.bfloat16),
            grad_mixed,
            preferred_element_type=jnp.float32,
        )
        grad_probs = jnp.einsum(
            "qhd,khd->hqk", grad_mixed, vals_rows, preferred_element_type=jnp.float32
        )
        grad_scores = (prob_rows * (grad_probs - delta_rows[..., None])).astype(jnp.bfloat16)
        carried = (
            carried
            + jnp.einsum("hqk,khd->qhd", grad_scores, keys_rows, preferred_element_type=jnp.float32)
            * scale_factor
        )
        grad_keys = (
            jnp.einsum("hqk,qhd->khd", grad_scores, query_rows, preferred_element_type=jnp.float32)
            * scale_factor
        )
        return (carried, (grad_keys, grad_vals))

    start_grad = jnp.zeros(query_rows.shape, jnp.float32)
    grad_query, (grad_keys, grad_vals) = lax.scan(
        grad_step, start_grad, (keys_blk, vals_blk, seg_blk)
    )
    return (grad_query, grad_keys, grad_vals)


def per_device(tokens, segment_ids, gain_attn, w_qkv, w_out, gain_ffn, w_up, w_down, cotangent):
    inputs = tokens[0].astype(jnp.float32)
    seg_mark = segment_ids[0] + 1
    row_count, feature_count = inputs.shape
    head_size = feature_count // HEADS
    normed_one, inverse_one = normalize(inputs)
    attn_in = (normed_one * gain_attn).astype(jnp.bfloat16)
    projected = jnp.dot(attn_in, w_qkv, preferred_element_type=jnp.float32).astype(jnp.bfloat16)
    query_rows = projected[:, :feature_count].reshape(row_count, HEADS, head_size)
    kv_local = projected[:, feature_count:]
    packed, seg_near = fetch_near(kv_local, seg_mark)
    keys_blk, vals_blk, seg_blk = split_blocks(packed, seg_near)
    mixed, logsum = attend_forward(query_rows, keys_blk, vals_blk, seg_blk, seg_mark)
    mixed_b = mixed.reshape(row_count, feature_count).astype(jnp.bfloat16)
    middle = inputs + jnp.dot(mixed_b, w_out, preferred_element_type=jnp.float32)
    normed_two, inverse_two = normalize(middle)
    ffn_in = (normed_two * gain_ffn).astype(jnp.bfloat16)
    hidden = jnp.dot(ffn_in, w_up, preferred_element_type=jnp.float32)
    active, gelu_back = jax.vjp(partial(jax.nn.gelu, approximate=False), hidden)
    active_b = active.astype(jnp.bfloat16)
    layer_out = middle + jnp.dot(active_b, w_down, preferred_element_type=jnp.float32)
    upstream_b = cotangent[0]
    upstream = upstream_b.astype(jnp.float32)
    grad_down = jnp.einsum("nf,nd->fd", active_b, upstream_b, preferred_element_type=jnp.float32)
    grad_active = jnp.einsum("nd,fd->nf", upstream_b, w_down, preferred_element_type=jnp.float32)
    grad_hidden = gelu_back(grad_active)[0].astype(jnp.bfloat16)
    grad_up = jnp.einsum("nd,nf->df", ffn_in, grad_hidden, preferred_element_type=jnp.float32)
    grad_ffn_in = jnp.einsum("nf,df->nd", grad_hidden, w_up, preferred_element_type=jnp.float32)
    grad_gain_ffn = jnp.sum(grad_ffn_in * normed_two, 0)
    grad_middle = upstream + norm_back(grad_ffn_in * gain_ffn, normed_two, inverse_two)
    grad_branch = grad_middle.astype(jnp.bfloat16)
    grad_out = jnp.einsum("nd,ne->de", mixed_b, grad_branch, preferred_element_type=jnp.float32)
    grad_mixed = jnp.einsum(
        "ne,de->nd", grad_branch, w_out, preferred_element_type=jnp.float32
    ).astype(jnp.bfloat16)
    grad_mixed = grad_mixed.reshape(row_count, HEADS, head_size)
    delta_rows = jnp.einsum("qhd,qhd->hq", grad_mixed.astype(jnp.float32), mixed)
    grad_query, grad_keys, grad_vals = attend_backward(
        query_rows, keys_blk, vals_blk, seg_blk, seg_mark, logsum, grad_mixed, delta_rows
    )
    near_rows = 3 * row_count
    kv_terms = jnp.concatenate(
        [grad_keys.reshape(near_rows, feature_count), grad_vals.reshape(near_rows, feature_count)],
        1,
    )
    lower_rim = kv_terms[:row_count]
    own_rows = kv_terms[row_count : 2 * row_count]
    upper_rim = kv_terms[2 * row_count :]
    from_right = from_behind(lower_rim.astype(jnp.bfloat16), "blk", -1).astype(lower_rim.dtype)
    from_left = from_behind(upper_rim.astype(jnp.bfloat16), "blk", 1).astype(upper_rim.dtype)
    kv_home = own_rows + from_right + from_left
    grad_proj = jnp.concatenate([grad_query.reshape(row_count, feature_count), kv_home], 1).astype(
        jnp.bfloat16
    )
    grad_qkv = jnp.einsum("nd,ne->de", attn_in, grad_proj, preferred_element_type=jnp.float32)
    grad_attn_in = jnp.einsum("ne,de->nd", grad_proj, w_qkv, preferred_element_type=jnp.float32)
    grad_gain_attn = jnp.sum(grad_attn_in * normed_one, 0)
    input_grad = grad_middle + norm_back(grad_attn_in * gain_attn, normed_one, inverse_one)
    part_qkv, part_out, part_up, part_down, part_gain_attn, part_gain_ffn = (
        lax.psum_scatter(
            grad_qkv.astype(jnp.bfloat16), "dp", scatter_dimension=0, tiled=True
        ).astype(jnp.float32),
        lax.psum_scatter(
            grad_out.astype(jnp.bfloat16), "dp", scatter_dimension=0, tiled=True
        ).astype(jnp.float32),
        lax.psum_scatter(
            grad_up.astype(jnp.bfloat16), "dp", scatter_dimension=0, tiled=True
        ).astype(jnp.float32),
        lax.psum_scatter(
            grad_down.astype(jnp.bfloat16), "dp", scatter_dimension=0, tiled=True
        ).astype(jnp.float32),
        lax.psum_scatter(
            grad_gain_attn.astype(jnp.bfloat16), "dp", scatter_dimension=0, tiled=True
        ).astype(jnp.float32),
        lax.psum_scatter(
            grad_gain_ffn.astype(jnp.bfloat16), "dp", scatter_dimension=0, tiled=True
        ).astype(jnp.float32),
    )
    sum_qkv, sum_out, sum_up, sum_down = (
        lax.psum_scatter(
            part_qkv.astype(jnp.bfloat16), "blk", scatter_dimension=1, tiled=True
        ).astype(jnp.float32),
        lax.psum_scatter(
            part_out.astype(jnp.bfloat16), "blk", scatter_dimension=1, tiled=True
        ).astype(jnp.float32),
        lax.psum_scatter(
            part_up.astype(jnp.bfloat16), "blk", scatter_dimension=1, tiled=True
        ).astype(jnp.float32),
        lax.psum_scatter(
            part_down.astype(jnp.bfloat16), "blk", scatter_dimension=1, tiled=True
        ).astype(jnp.float32),
    )
    total_gain_attn, total_gain_ffn = lax.psum((part_gain_attn, part_gain_ffn), "blk")
    return (
        layer_out[None],
        input_grad[None],
        total_gain_attn,
        sum_qkv,
        sum_out,
        total_gain_ffn,
        sum_up,
        sum_down,
    )


def copy_kernel(count, *refs):
    source, target, held = refs[:count], refs[count : 2 * count], refs[2 * count : 3 * count]
    sems = refs[3 * count]
    pieces = []
    for k in range(count):
        rows = source[k].shape[0]
        step = rows // 4 if rows % 64 == 0 else rows
        pieces += [(k, pl.ds(at, step)) for at in range(0, rows, step)]
    loads = [pltpu.make_async_copy(source[k].at[at], held[k].at[at], sems.at[0, n]) for n, (k, at) in enumerate(pieces)]
    stores = [pltpu.make_async_copy(held[k].at[at], target[k].at[at], sems.at[1, n]) for n, (k, at) in enumerate(pieces)]
    for copy in loads:
        copy.start()
    for load, store in zip(loads, stores):
        load.wait()
        store.start()
    for copy in stores:
        copy.wait()


def copy_out(arrays):
    anywhere = pl.BlockSpec(memory_space=pl.ANY)
    return pl.pallas_call(
        partial(copy_kernel, len(arrays)),
        out_shape=[jax.ShapeDtypeStruct(a.shape, a.dtype) for a in arrays],
        in_specs=[anywhere] * len(arrays),
        out_specs=[anywhere] * len(arrays),
        scratch_shapes=[pltpu.VMEM(a.shape, a.dtype) for a in arrays]
        + [pltpu.SemaphoreType.DMA((2, 4 * len(arrays)))],
        name="copy_out",
    )(*arrays)


def fast(tokens, segment_ids, gain_attn, w_qkv, w_out, gain_ffn, w_up, w_down, cotangent):
    x, cot = tokens[0], cotangent[0]
    rows, width = x.shape
    layer_out, input_grad, gains, g_qkv, g_out, g_up, g_down = call_layer(
        x, segment_ids, gain_attn.reshape(-1, TILE), gain_ffn.reshape(-1, TILE), w_qkv, w_out, w_up, w_down, cot
    )
    layer_out, input_grad, g_qkv, g_out, g_up, g_down = copy_out(
        [layer_out, input_grad, g_qkv, g_out, g_up, g_down]
    )
    block = width // 16
    mine = lax.dynamic_slice(gains[5], (0, lax.axis_index("dp") * block), (2, block))
    return (layer_out[None], input_grad[None], mine[1], g_qkv, g_out, mine[0], g_up, g_down)


def fits(mesh, tokens, w_qkv, w_up):
    rows, width, ff = tokens.shape[1] // mesh.shape["blk"], tokens.shape[2], w_up.shape[1]
    return (
        mesh.shape["dp"] == 16 and mesh.shape["blk"] == 2 and tokens.shape[0] == 16
        and rows % TILE == 0 and rows <= 640 and (rows - min(rows, REACH)) % 64 == 0
        and width == HEADS * 64 and ff == 4 * width
    )


def solution(mesh):
    def program(*args):
        body = fast if fits(mesh, args[0], args[3], args[6]) else per_device
        rows, whole = P("dp", "blk", None), P()
        return jax.shard_map(
            body,
            mesh=mesh,
            in_specs=(rows, P("dp", "blk"), whole, whole, whole, whole, whole, whole, rows),
            out_specs=(rows, rows, P("dp"), P("dp", "blk"), P("dp", "blk"), P("dp"), P("dp", "blk"), P("dp", "blk")),
            check_vma=False,
        )(*args)

    return program
```

```python
from functools import partial
import math
from types import SimpleNamespace

import jax
import jax.numpy as jnp
from jax import lax
from jax.experimental import pallas as pl
from jax.experimental.pallas import tpu as pltpu
from jax.sharding import PartitionSpec as P

HEADS = 12
NEG = -1e30
LOG2E = math.log2(math.e)
IMAGES = (197, 577)
REACH = 576
TILE = 128
UNIT = 128
F32, BF16 = jnp.float32, jnp.bfloat16
MESH = pl.DeviceIdType.MESH
NN = (((1,), (0,)), ((), ()))
NT = (((1,), (1,)), ((), ()))
BITS = ("core", "x", "z0", "z1", "y")
ORDER_A = ("core", "x", "y", "z0", "z1")
ORDER_B = ("core", "z0", "z1", "x", "y")
ORDER_C = ("core", "y", "x", "z0", "z1")
ORDER_D = ("core", "z0", "z1", "y", "x")
ORDER_E = ("core", "x", "z0", "z1", "y")
OUT_AFTER = 5
ORDERS = (ORDER_C, ORDER_E, ORDER_C, ORDER_E, ORDER_C, ORDER_E, ORDER_A, ORDER_E, ORDER_D, ORDER_C, ORDER_C, ORDER_D, ORDER_A, ORDER_D, ORDER_A, ORDER_D, ORDER_A)
ENDS = {
    ("ff", 2): ((0, 0), (1, 0),),
    ("ff", 4): ((0, 1), (2, 0), (3, 0),),
    ("dn", 1): ((2, 1),),
    ("dn", 2): ((3, 1), (4, 0), (5, 0),),
    ("gm", 0): ((0, 2), (1, 1),),
    ("de", 0): ((2, 2),),
    ("own", 0): ((0, 3), (2, 3), (1, 2), (3, 2), (4, 1), (5, 1), (6, 0),),
    ("own", 1): ((8, 0),),
    ("own", 2): ((0, 4), (2, 4), (1, 3), (3, 3), (4, 2), (5, 2), (7, 0),),
    ("own", 3): ((1, 4), (3, 4), (4, 3), (5, 3), (6, 1),),
    ("own", 4): ((4, 4), (5, 4), (8, 1),),
    ("out", 0): ((7, 1),),
    ("own", 5): ((6, 2), (9, 0),),
    ("oth", 2): ((7, 2), (8, 2),),
    ("oth", 3): ((6, 3), (9, 1),),
    ("oth", 4): ((8, 3), (10, 0), (11, 0), (12, 0),),
    ("oth", 5): ((6, 4), (7, 3), (9, 2), (13, 0), (14, 0),),
    ("tail", 0): ((8, 4), (11, 1), (12, 1), (15, 0), (16, 0),),
    ("tail", 1): ((7, 4), (9, 3), (14, 1),),
    ("tail", 2): ((13, 1),),
    ("tail", 4): ((12, 2), (10, 1),),
    ("tail", 5): ((16, 1),),
    ("tail", 6): ((11, 2),),
    ("tail", 7): ((14, 2), (9, 4), (11, 3), (12, 3), (16, 2), (15, 1), (14, 3), (10, 2), (13, 2), (11, 4), (12, 4), (16, 3), (13, 3), (14, 4), (13, 4), (16, 4), (15, 2), (10, 3), (15, 3), (10, 4), (15, 4),),
}


def dot(a, b, dims=NN):
    return lax.dot_general(a, b, dims, preferred_element_type=F32)


def aligned(value, unit):
    return pl.multiple_of(value, unit)


def tile_at(index):
    return pl.ds(aligned(index * TILE, TILE), TILE)


def chunks(total, size):
    return [(at, min(size, total - at)) for at in range(0, total, size)]


def interleave(first, second):
    first, second = list(first), list(second)
    done = 0
    for k, step in enumerate(first):
        step()
        upto = (k + 1) * len(second) // len(first)
        for other in second[done:upto]:
            other()
        done = upto
    for other in second[done:]:
        other()


def pipeline(before, during, after):
    count = len(during)
    for step in before[0]:
        step()
    for n in range(count):
        matrix = (list(after[n - 1]) if n else []) + (list(before[n + 1]) if n + 1 < count else [])
        interleave(matrix, during[n])
    for step in after[count - 1]:
        step()


def pair_rows(slab):
    first = lax.broadcasted_iota(jnp.int32, slab.shape, 1) < slab.shape[1] // 2
    zero = jnp.zeros_like(slab)
    return jnp.concatenate([jnp.where(first, slab, zero), jnp.where(first, zero, slab)], 0)


def own_halves(block):
    half = TILE // 2
    return jnp.concatenate([block[:half, :TILE], block[half:TILE, TILE:]], 0)


def fold_sum(block):
    return jnp.sum(block.reshape(block.shape[0] // 8, 8, block.shape[1]), 0)


def standardize(values):
    mean = jnp.mean(values, -1, keepdims=True)
    centered = values - mean
    variance = jnp.mean(centered * centered, -1, keepdims=True)
    inverse = lax.rsqrt(variance + 1e-05)
    return centered * inverse, inverse


def norm_backward(grad, normed, inverse):
    first = jnp.mean(grad, -1, keepdims=True)
    second = jnp.mean(grad * normed, -1, keepdims=True)
    return inverse * (grad - first - normed * second)


def near_keys(rows, t):
    return max(0, min(rows, REACH) - TILE * t)


def by_row_tiles(rows, body):
    def tile(i, _):
        for part in range(0, TILE, 32):
            body(pl.ds(aligned(i * TILE + part, 32), 32))
        return 0

    lax.fori_loop(0, rows // TILE, tile, 0)


def border_rows(rows):
    starts, found = {0}, {0}
    while found:
        found = {at + size for at in found for size in IMAGES if at + size < rows} - starts
        starts |= found
    reach = max(max(rows - at, at + size - rows) for at in starts for size in IMAGES if at < rows < at + size)
    return min(rows, -(-reach // 16) * 16)


def mark_segments(seg_ref, keys_ref, queries_ref, rows):
    for at, size in chunks(rows, TILE):
        column = jnp.broadcast_to(seg_ref[0:1, at : at + size].astype(F32), (TILE, size)).T
        same = column == lax.broadcasted_iota(jnp.int32, (size, TILE), 1).astype(F32)
        keys_ref[at : at + size, :] = jnp.where(same, 1.0, 0.0).astype(BF16)
        queries_ref[at : at + size, :] = jnp.where(same, 0.0, NEG).astype(BF16)


def both_rows(block):
    return jnp.concatenate([block, block], 0)


def with_marks(slab, marks):
    return jnp.concatenate([slab, marks], 1)


def shared_steps(sizes, most):
    groups = []
    for t, size in sorted(enumerate(sizes), key=lambda item: -item[1]):
        if not size:
            continue
        for group in groups:
            if sum(sizes[other] for other in group) + size <= most:
                group.append(t)
                break
        else:
            groups.append([t])
    return groups


def row_of(gain_ref):
    return jnp.concatenate([gain_ref[i : i + 1, :] for i in range(gain_ref.shape[0])], 1)


def norm_rows(x_ref, gain_ref, out_ref, rows, row_from=0):
    def tile(i, _):
        for part in range(0, 64, 32):
            at = pl.ds(aligned(row_from + i * 64 + part, 32), 32)
            normed, _ = standardize(x_ref[at, :].astype(F32))
            out_ref[at, :] = (normed * row_of(gain_ref)).astype(BF16)
        return 0

    lax.fori_loop(0, rows // 64, tile, 0)


def transpose_steps(src, base, into, row_from, count, width):
    def one(c, at, part):
        def step():
            rows_here = pl.ds(row_from + at if isinstance(row_from, int) else aligned(row_from + at, 64), part)
            into[c : c + TILE, at : at + part] = src[rows_here, base + c : base + c + TILE].T

        return step

    return [one(c, at, part) for c in range(0, width, TILE) for at, part in chunks(count, TILE)]


def project(a_ref, w_ref, out_ref, width, at, after_values):
    def one(c):
        def step():
            scale = 0.125 * LOG2E if c < width else 1.0
            out_ref[at, c : c + 256] = (dot(a_ref[at, :], w_ref[:, c : c + 256]) * scale).astype(BF16)

        return step

    for c in range(2 * width, 3 * width, 256):
        one(c)()
    interleave([one(c) for c in range(0, 2 * width, 256)], after_values)


def own_tile(t, tiles, me):
    return (tiles - 1 - t) * (1 - me) + t * me


def softmax_steps(items, scores_ref, probs_ref):
    count = len(items)

    def here(n, block, at, size):
        return slice(block["off"] + at, block["off"] + at + size), slice((n % 2) * 256, (n % 2) * 256 + 256)

    def scores(n):
        def one(block):
            def step():
                scores_ref[block["lane"]][here(n, block, 0, block["size"])] = dot(block["k"](), block["q2"](), NT)

            return step

        return [one(block) for block in items[n]]

    def largest(n):
        steps = []
        for block in items[n]:

            def part(at, block=block):
                def step():
                    new = scores_ref[block["lane"]][here(n, block, at, 32)]
                    block["max"] = jnp.maximum(block["max"], new) if at else new

                return step

            def last(block=block):
                top = jnp.max(block["max"], 0, keepdims=True)
                was = block["top"]()
                block["max"] = top if was is None else jnp.maximum(top, was)

            steps += [part(at) for at in range(0, block["size"], 32)] + [last]
        return steps

    def exponentials(n):
        def part(block, at, size):
            def step():
                s = scores_ref[block["lane"]][here(n, block, at, size)]
                probs_ref[block["lane"]][here(n, block, at, size)] = jnp.exp2(s - block["max"]).astype(BF16)

            return step

        return [part(block, at, size) for block in items[n] for at, size in chunks(block["size"], 64)]

    def values(n):
        def one(block):
            def step():
                vt = jnp.concatenate([block["vt"](), jnp.ones((16, block["size"]), BF16)], 0)
                mix = dot(vt, probs_ref[block["lane"]][here(n, block, 0, block["size"])])
                block["end"](block["max"], mix[TILE : TILE + 1, :], own_halves(mix))

            return step

        return [one(block) for block in items[n]]

    for step in scores(0) + largest(0):
        step()
    for n in range(count):
        interleave(scores(n + 1) if n + 1 < count else [], exponentials(n))
        interleave(values(n), largest(n + 1) if n + 1 < count else [])


def attend_local(r, rows, width):
    tiles, half_pairs = rows // TILE, width // TILE // 2

    def two_pairs(first, _):
        def one(k, u):
            hp = first + k * half_pairs
            lane = lambda base: pl.ds(aligned(base + hp * TILE, TILE), TILE)
            row_u = slice(u * TILE, u * TILE + TILE)

            def end(top, total, mix):
                r.top[pl.ds(hp * tiles + u, 1), :] = top
                r.total[pl.ds(hp * tiles + u, 1), :] = total
                r.gf[row_u, lane(0)] = mix

            return dict(
                size=rows, off=0, lane=k, top=lambda: None, end=end,
                q2=lambda: with_marks(pair_rows(r.pv[row_u, lane(0)]), both_rows(r.seg_q[row_u, :])),
                k=lambda: with_marks(r.pv[:, lane(width)], r.seg_k[...]),
                vt=lambda: r.act_t[lane(0), :rows],
            )

        softmax_steps([[one(k, u) for k in range(2)] for u in range(tiles)], (r.h, r.ga), (r.act, r.gh))
        return 0

    lax.fori_loop(0, half_pairs, two_pairs, 0)


def attend_cross(r, me, rows, width):
    tiles, half_pairs = rows // TILE, width // TILE // 2
    sizes = [near_keys(rows, t) for t in range(tiles)]

    def two_pairs(first, _):
        def one(k, t, off):
            hp = first + k * half_pairs
            lane = lambda base: pl.ds(aligned(base + hp * TILE, TILE), TILE)
            size = sizes[t]
            u = own_tile(t, tiles, me)
            i = hp * tiles + u
            keys = pl.ds(aligned((rows - size) * me, 64), size)
            lanes = pl.ds(aligned(TILE * t * me, TILE), size)

            def end(top, total, mix):
                top_was, total_was = r.top[pl.ds(i, 1), :], r.total[pl.ds(i, 1), :]
                fade = jnp.exp2(top_was - top)
                total = total_was * fade + total
                over = 1.0 / total
                half = TILE // 2
                by_head = lambda row: jnp.concatenate(
                    [jnp.broadcast_to(row[:, :TILE], (half, TILE)), jnp.broadcast_to(row[:, TILE:], (half, TILE))], 0
                )
                done = (r.gf[tile_at(u), lane(0)] * by_head(fade) + mix) * by_head(over)
                r.mixedv[tile_at(u), lane(0)] = done.T.astype(BF16)
                r.stats[0, pl.ds(hp * tiles + t, 1), :] = top + jnp.log2(total)

            return dict(
                size=size, off=off, lane=k, top=lambda: r.top[pl.ds(i, 1), :], end=end,
                q2=lambda: with_marks(pair_rows(r.pv[tile_at(u), lane(0)]), both_rows(r.seg_q[tile_at(u), :])),
                k=lambda: with_marks(r.prv[keys, lane(width)], r.seg_kr[keys, :]),
                vt=lambda: r.act_t[pl.ds(aligned(width + hp * TILE, TILE), TILE), lanes],
            )

        items = []
        for group in shared_steps(sizes, rows):
            offs = [sum(sizes[other] for other in group[:n]) for n in range(len(group))]
            items.append([one(k, t, off) for t, off in zip(group, offs) for k in range(2)])
        softmax_steps(items, (r.h, r.ga), (r.act, r.gh))

        for t in range(tiles):
            if not sizes[t]:
                for k in range(2):
                    no_neighbour(first + k * half_pairs, t)
        return 0

    def no_neighbour(hp, t):
        lane = pl.ds(aligned(hp * TILE, TILE), TILE)
        u = own_tile(t, tiles, me)
        i = hp * tiles + u
        total = r.total[pl.ds(i, 1), :]
        over = 1.0 / total
        half = TILE // 2
        scale = jnp.concatenate(
            [jnp.broadcast_to(over[:, :TILE], (half, TILE)), jnp.broadcast_to(over[:, TILE:], (half, TILE))], 0
        )
        r.mixedv[tile_at(u), lane] = (r.gf[tile_at(u), lane] * scale).T.astype(BF16)
        r.stats[0, pl.ds(hp * tiles + t, 1), :] = r.top[pl.ds(i, 1), :] + jnp.log2(total)

    lax.fori_loop(0, half_pairs, two_pairs, 0)


INV_SQRT2PI = 1.0 / math.sqrt(2.0 * math.pi)
TAIL_SLOPE = 0.3275911 * math.sqrt(0.5)
TAIL = tuple(0.5 * c for c in (0.254829592, -0.284496736, 1.421413741, -1.453152027, 1.061405429))


def gelu_parts(h):
    below_one = 1.0 + TAIL_SLOPE * jnp.abs(h)
    t = pl.reciprocal(below_one, approx=True)
    t = t * (2.0 - below_one * t)
    bell = jnp.exp2(h * h * (-0.5 * LOG2E))
    poly = TAIL[4]
    for c in TAIL[3::-1]:
        poly = poly * t + c
    tail = poly * t * bell
    below = jnp.where(h < 0.0, tail, 1.0 - tail)
    return below, below + h * bell * INV_SQRT2PI


def where_am_i():
    dp, blk = lax.axis_index("dp"), lax.axis_index("blk")
    bits = {name: lax.rem(lax.div(dp, 2**k), 2) for k, name in enumerate(BITS[:-1])}
    bits["y"] = blk
    return dp, blk, bits


def partner_of(name, dp, blk, bits):
    if name == "y":
        return {"blk": 1 - blk}
    return {"dp": dp + 2 ** BITS.index(name) * (1 - 2 * bits[name])}


def block_index(order, d, y):
    bits = {name: (d >> k) & 1 for k, name in enumerate(BITS[:-1])}
    bits["y"] = y
    index = 0
    for name in order:
        index = 2 * index + bits[name]
    return index


class Reducer:
    def __init__(self, r):
        self.r = r
        self.dp, self.blk, self.bits = where_am_i()

    def keep(self, order, stage):
        base = 0
        for k in range(stage + 1):
            base = base + self.bits[order[k]] * (16 >> k)
        return base

    def copy(self, chunk, stage):
        number, unit, units, order, _ = chunk
        half = 16 >> stage
        base = self.keep(order, stage - 1) if stage else 0
        away = base + (1 - self.bits[order[stage]]) * half
        slot = 32 - 2 * half
        return pltpu.make_async_remote_copy(
            src_ref=self.r.g.at[pl.ds(unit, units), pl.ds(away, half)],
            dst_ref=self.r.recv.at[pl.ds(unit, units), pl.ds(slot, half)],
            send_sem=self.r.rs_sent.at[number, stage],
            recv_sem=self.r.rs_got.at[number, stage],
            device_id=partner_of(order[stage], self.dp, self.blk, self.bits),
            device_id_type=MESH,
        )

    def start(self, chunk, stage=0):
        self.copy(chunk, stage).start()

    def finish(self, chunk, stage):
        number, unit, units, order, write = chunk
        half = 16 >> stage
        self.copy(chunk, stage).wait()
        keep = self.keep(order, stage)
        slot = 32 - 2 * half
        if stage == 4:
            for k in range(units):
                write(k, self.r.g[unit + k, keep].astype(F32) + self.r.recv[unit + k, slot].astype(F32))
            return
        step = min(half, 4)

        def add(j, _):
            for k in range(units):
                mine = pl.ds(keep + j * step, step)
                self.r.g[unit + k, mine] += self.r.recv[unit + k, pl.ds(slot + j * step, step)]
            return 0

        if half == step:
            add(0, 0)
        else:
            lax.fori_loop(0, half // step, add, 0)
        self.start(chunk, stage + 1)


def kernel_layer(names, *refs):
    r = SimpleNamespace(**dict(zip(names, refs)))
    rows, width = r.xv.shape
    ff = r.wb.shape[0]
    me = lax.axis_index("blk")
    reach, tiles, pairs = min(rows, REACH), rows // TILE, width // TILE
    red = Reducer(r)
    dp, blk, bits = red.dp, red.blk, red.bits

    barrier = pltpu.get_barrier_semaphore()
    for name in BITS:
        pl.semaphore_signal(
            barrier, inc=1, device_id=partner_of(name, dp, blk, bits), device_id_type=MESH
        )
    loads = {}
    for k, (src, into) in enumerate(
        [("x", r.xv), ("w_qkv", r.wa.at[:, : 3 * width]), ("w_out", r.wo), ("cot", r.cotv), ("w_down", r.wb)]
    ):
        loads[src] = pltpu.make_async_copy(getattr(r, src), into, r.loads.at[k])
        loads[src].start()
    loads["w_up"] = pltpu.make_async_copy(r.w_up, r.wa, r.loads.at[5])
    load_w_qkv = pltpu.make_async_copy(r.w_qkv, r.wa.at[:, : 3 * width], r.loads.at[6])
    near, span = rows // 2, border_rows(rows)
    far = pl.ds(aligned(span * (1 - me), 16), rows - span)
    give = pl.ds(aligned((rows - span) * (1 - me), 16), span)
    give_near = pl.ds(aligned((rows - near) * (1 - me), 16), near)
    give_far = pl.ds(aligned((rows - span) * (1 - me) + near * me, 16), span - near)
    to_y = dict(device_id={"blk": 1 - me}, device_id_type=MESH)
    if span < rows:
        r.xr[far, :] = jnp.zeros((rows - span, width), BF16)
        r.gmr[far, :] = jnp.zeros((rows - span, width), BF16)
    loads["x"].wait()
    pl.semaphore_wait(barrier, len(BITS))

    def to_neighbour(k, src, dst):
        copy = pltpu.make_async_remote_copy(
            src_ref=src, dst_ref=dst, send_sem=r.sent.at[k], recv_sem=r.got.at[k], **to_y
        )
        copy.start()
        return copy

    send_near = to_neighbour(0, r.xv.at[give_near], r.xr.at[give_near])
    send_seg = to_neighbour(1, r.seg, r.segr)
    send_far = to_neighbour(4, r.xv.at[give_far], r.xr.at[give_far])
    norm_rows(r.xv, r.gain_attn, r.ffn_in, rows)
    mark_segments(r.seg, r.seg_k, r.seg_q, rows)
    loads["w_qkv"].wait()
    project(r.ffn_in, r.wa, r.pv, width, slice(None), transpose_steps(r.pv, 2 * width, r.act_t, 0, rows, width))
    attend_local(r, rows, width)

    send_seg.wait()
    mark_segments(r.segr, r.seg_kr, r.seg_qr, rows)

    def neighbour_half(n, _):
        pl.when(n == 0)(send_near.wait)
        pl.when(n == 1)(send_far.wait)
        row_from = near * (me * (1 - n) + (1 - me) * n)
        norm_rows(r.xr, r.gain_attn, r.ffn_in, near, row_from)
        project(r.ffn_in, r.wa, r.prv, width, pl.ds(aligned(row_from, 64), near), [])
        return 0

    lax.fori_loop(0, 2, neighbour_half, 0)
    loads["w_up"].start()
    for step in transpose_steps(r.prv, 2 * width, r.act_t.at[width : 2 * width, :], (rows - reach) * me, reach, width):
        step()
    attend_cross(r, me, rows, width)

    block_rows = width // 16

    def put(unit, order, d, y, row, block):
        r.g[unit, block_index(order, d, y), row : row + block.shape[0], :] = block

    def into(ref, base):
        def write(k, block):
            ref[:, tile_at(base + k)] = block

        return write


    def up_unit(i, k):
        return lax.div(i, 2) * 4 + 2 * k + lax.rem(i, 2) if not isinstance(i, int) else i // 2 * 4 + 2 * k + i % 2

    def chunk_up(c, k):
        def write(m, block):
            r.o_up[:, tile_at(4 * c + 2 * m + k)] = block

        return (2 * c + k, 4 * c + 2 * k, 2, ORDERS[k], write)

    def chunk_down(j):
        def write(k, block):
            r.o_down[k * block_rows : (k + 1) * block_rows, j * UNIT : (j + 1) * UNIT] = block

        return (6 + j, 12 + 4 * j, 4, ORDERS[6 + j], write)

    out_chunk = (9, 0, 3, ORDERS[9], into(r.o_out, 0))

    middle_chunk = (10, 6, 3, ORDERS[10], into(r.o_qkv, 3))

    def chunk_qkv(n, k):
        j = n + 6 * k
        return (11 + 2 * n + k, 3 + j, 1, ORDERS[11 + k], into(r.o_qkv, j))

    table = [chunk_up(c, k) for c in range(3) for k in range(2)] + [chunk_down(j) for j in range(3)]
    table += [out_chunk, middle_chunk] + [chunk_qkv(n, k) for n in range(3) for k in range(2)]

    def ends(name, step):
        for chunk, stage in ENDS.get((name, step), ()):
            red.finish(table[chunk], stage)

    def ends_in_loop(name, index, steps):
        for step in steps:
            if (name, step) in ENDS:
                pl.when(index == step)(lambda step=step: ends(name, step))

    loads["w_out"].wait()
    for c, part in chunks(width, 256):
        r.mid[:, c : c + part] = r.xv[:, c : c + part].astype(F32) + dot(r.mixedv[...], r.wo[:, c : c + part])

    def norm_two(at):
        normed, _ = standardize(r.mid[at, :])
        r.ffn_in[at, :] = (normed * row_of(r.gain_ffn)).astype(BF16)
        r.lo[at, :] = r.mid[at, :]
        r.gf[at, :] = jnp.zeros_like(r.gf[at, :])

    norm_two_steps = [lambda at=at: norm_two(slice(at, at + 32)) for at in range(0, rows, 32)]
    norm_two_steps += transpose_steps(r.ffn_in, 0, r.ffn_t, 0, rows, width)
    for src in ("w_up", "cot", "w_down"):
        loads[src].wait()

    def column(n, i):
        return pl.ds(aligned((n % 2) * (ff // 2) + i * 256, 256), 256)

    def side(n):
        return slice((n % 2) * 256, (n % 2) * 256 + 256)

    def ff_before(n, i):
        def up():
            r.h[:, side(n)] = dot(r.ffn_in[...], r.wa[:, column(n, i)])

        def down():
            r.ga[:, side(n)] = dot(r.cotv[...], r.wb[column(n, i), :], NT)

        return [up, down]

    def ff_during(n):
        def part(row):
            def step():
                tile = slice(row, row + 32)
                h = r.h[tile, side(n)]
                below, slope = gelu_parts(h)
                r.act[tile, side(n)] = (h * below).astype(BF16)
                r.gh[tile, side(n)] = (slope * r.ga[tile, side(n)]).astype(BF16)

            return step

        return [part(row) for row in range(0, rows, 32)]

    def ff_after(n, i):
        def out(c):
            def step():
                r.lo[:, c : c + 256] += dot(r.act[:, side(n)], r.wb[column(n, i), c : c + 256])

            return step

        def back(c):
            def step():
                r.gf[:, c : c + 256] += dot(r.gh[:, side(n)], r.wa[c : c + 256, column(n, i)], NT)

            return step

        def weights():
            grad = dot(r.ffn_t[...], r.gh[:, side(n)]).astype(BF16)
            for d in range(16):
                for k in range(2):
                    put(up_unit(i, k), ORDERS[k], d, n % 2, 0,
                        grad[d * block_rows : (d + 1) * block_rows, k * UNIT : (k + 1) * UNIT])

        def turn():
            base = (n % 2) * (ff // 2) + i * 256
            for c in range(0, 256, TILE):
                for row in range(0, rows, TILE):
                    r.act_t[pl.ds(aligned(base + c, TILE), TILE), row : row + TILE] = r.act[
                        row : row + TILE, (n % 2) * 256 + c : (n % 2) * 256 + c + TILE].T

        return [weights] + [step(c) for step in (out, back) for c in range(0, width, 256)] + [turn]

    last = ff // 512 - 1
    interleave([ff_before(0, 0)[1], ff_before(1, 0)[1]], norm_two_steps)
    ff_before(0, 0)[0]()
    interleave(ff_before(1, 0)[:1], ff_during(0))

    def ff_two(i, _):
        interleave(ff_after(0, i) + ff_before(0, i + 1), ff_during(1))
        interleave(ff_after(1, i) + ff_before(1, i + 1), ff_during(0))

        @pl.when(lax.rem(i, 2) == 1)
        def _():
            for k in range(2):
                red.start(chunk_up(lax.div(i, 2), k))

        ends_in_loop("ff", i, range(last))
        return 0

    lax.fori_loop(0, last, ff_two, 0)
    interleave(ff_after(0, last), ff_during(1))
    for step in ff_after(1, last):
        step()
    for k in range(2):
        red.start(chunk_up(last // 2, k))
    ends("ff", last)
    load_w_qkv.start()
    out_lo = pltpu.make_async_copy(r.lo, r.layer_out, r.loads.at[7])
    out_lo.start()

    def grad_down(j):
        order = ORDERS[6 + j]

        def part(c):
            def step():
                both = jnp.concatenate(
                    [r.cotv[:, half * (width // 2) + j * UNIT : half * (width // 2) + (j + 1) * UNIT]
                     for half in range(2)], 1)
                grad = dot(r.act_t[c : c + width, :], both).astype(BF16)
                for part in range(4):
                    for k in range(4):
                        for half in range(2):
                            at = part * 4 * block_rows + k * block_rows
                            put(12 + 4 * j + k, order, 4 * (c // width) + part, half, 0,
                                grad[at : at + block_rows, half * UNIT : (half + 1) * UNIT])

            return step

        return [part(c) for c in range(0, ff, width)]

    r.gains[...] = jnp.zeros_like(r.gains)

    def norm_two_back(at):
        def step():
            normed, inverse = standardize(r.mid[at, :])
            grad = r.gf[at, :]
            r.gains[0:8, :] += fold_sum(grad * normed)
            grad = r.cotv[at, :].astype(F32) + norm_backward(
                grad * row_of(r.gain_ffn), normed, inverse
            )
            r.gf[at, :] = grad
            r.ffn_in[at, :] = grad.astype(BF16)

        return step

    def norm_one_again(at):
        def step():
            normed, _ = standardize(r.xv[at, :].astype(F32))
            r.xr[at, :] = (normed * row_of(r.gain_attn)).astype(BF16)

        return step

    row_tiles = [slice(at, at + 32) for at in range(0, rows, 32)]
    beside = [
        [norm_two_back(at) for at in row_tiles],
        [norm_one_again(at) for at in row_tiles] + transpose_steps(r.mixedv, 0, r.ffn_t, 0, rows, width),
        transpose_steps(r.xr, 0, r.n1_t, 0, rows, width) + transpose_steps(r.pv, width, r.kt, 0, rows, width)
        + transpose_steps(r.prv, width, r.ktr, (rows - reach) * me, reach, width),
    ]
    for j in range(3):
        for n, step in enumerate(grad_down(j)):
            share = beside[j][n * len(beside[j]) // 4 : (n + 1) * len(beside[j]) // 4]
            pl.when(me >= 0)(lambda step=step, share=share: interleave([step], share))
        red.start(chunk_down(j))
        ends("dn", j)

    for c, part in chunks(width, 256):
        r.gm[:, c : c + part] = dot(r.ffn_in[...], r.wo[c : c + part, :], NT).astype(BF16)
    send_gm = to_neighbour(2, r.gm.at[give], r.gmr.at[give])
    ends("gm", 0)

    def delta_rows(hp, _):
        lane = tile_at(hp)
        half = TILE // 2
        for t in range(tiles):
            at = tile_at(own_tile(t, tiles, me))
            both = (r.gm[at, lane].astype(F32) * r.mixedv[at, lane].astype(F32)).T
            first = jnp.sum(both[:half, :], 0, keepdims=True)
            second = jnp.sum(both[half:, :], 0, keepdims=True)
            r.stats[1, pl.ds(hp * tiles + t, 1), :] = jnp.concatenate([first, second], 1)
        return 0

    lax.fori_loop(0, pairs, delta_rows, 0)
    send_stats = to_neighbour(3, r.stats, r.statsr)
    ends("de", 0)

    out_lo.wait()

    def grad_steps(items):
        def here(n, block, at, size):
            return slice(block["off"] + at, block["off"] + at + size), side(n)

        def before(n):
            def scores(block):
                def step():
                    r.h[here(n, block, 0, block["size"])] = dot(block["k"](), block["q2"](), NT)

                return step

            def probs(block):
                def step():
                    r.ga[here(n, block, 0, block["size"])] = dot(block["v"](), block["do2"](), NT)

                return step

            return [step(block) for block in items[n] for step in (scores, probs)]

        def during(n):
            def part(block, at, size):
                def step():
                    rows_here = here(n, block, at, size)
                    p = jnp.exp2(r.h[rows_here] - block["lse"]())
                    r.act[rows_here] = p.astype(BF16)
                    r.gh[rows_here] = (p * (r.ga[rows_here] - block["delta"]())).astype(BF16)

                return step

            return [part(block, at, size) for block in items[n] for at, size in chunks(block["size"], 64)]

        def after(n):
            steps = []
            for block in items[n]:
                rows_here = here(n, block, 0, block["size"])
                steps += block["after"](lambda at=rows_here: r.act[at], lambda at=rows_here: r.gh[at])
            return steps

        count = range(len(items))
        pipeline([before(n) for n in count], [during(n) for n in count], [after(n) for n in count])

    sizes = [near_keys(rows, t) for t in range(tiles)]
    groups = shared_steps(sizes, rows)

    def offsets(group):
        return [(t, sum(sizes[other] for other in group[:n])) for n, t in enumerate(group)]

    def own_queries(hp):
        lane = lambda base: pl.ds(aligned(base + hp * TILE, TILE), TILE)
        parts = [[] for _ in range(tiles)]

        def base(t):
            at_u = tile_at(own_tile(t, tiles, me))
            return dict(
                q2=lambda: with_marks(pair_rows(r.pv[at_u, lane(0)]), both_rows(r.seg_q[at_u, :])),
                do2=lambda: pair_rows(r.gm[at_u, lane(0)]),
                lse=lambda: r.stats[0, pl.ds(hp * tiles + t, 1), :],
                delta=lambda: r.stats[1, pl.ds(hp * tiles + t, 1), :],
            )

        def add_queries(t, new):
            parts[t].append(new)
            if len(parts[t]) == (2 if sizes[t] else 1):
                dq = own_halves(sum(parts[t][1:], parts[t][0])) * 0.125
                r.mixedv[tile_at(own_tile(t, tiles, me)), lane(0)] = dq.T.astype(BF16)

        def local(t):
            mine = base(t)

            def after(p, ds):
                def queries():
                    add_queries(t, dot(r.kt[lane(0), :], ds()))

                def values():
                    new = dot(p(), mine["do2"]())
                    r.mid[:, lane(0)] = new if t == 0 else r.mid[:, lane(0)] + new

                def keys():
                    new = dot(ds(), pair_rows(r.pv[tile_at(own_tile(t, tiles, me)), lane(0)]))
                    r.lo[:, lane(0)] = new if t == 0 else r.lo[:, lane(0)] + new

                return [queries, values, keys]

            return dict(mine, size=rows, off=0, after=after, v=lambda: r.pv[:, lane(2 * width)],
                        k=lambda: with_marks(r.pv[:, lane(width)], r.seg_k[...]))

        def cross(t, off):
            keys = pl.ds(aligned((rows - sizes[t]) * me, 64), sizes[t])
            lanes = pl.ds(aligned(TILE * t * me, TILE), sizes[t])

            def after(p, ds):
                def queries():
                    add_queries(t, dot(r.ktr[lane(0), lanes], ds()))

                return [queries]

            return dict(base(t), size=sizes[t], off=off, after=after, v=lambda: r.prv[keys, lane(2 * width)],
                        k=lambda: with_marks(r.prv[keys, lane(width)], r.seg_kr[keys, :]))

        items = []
        for t in range(tiles):
            items.append([local(t)])
            if t < len(groups):
                items.append([cross(other, off) for other, off in offsets(groups[t])])
        grad_steps(items)

    def other_queries(hp):
        lane = lambda base: pl.ds(aligned(base + hp * TILE, TILE), TILE)

        def block(t, off):
            at_u = tile_at(t * (1 - me) + (tiles - 1 - t) * me)
            keys = pl.ds(aligned((rows - sizes[t]) * (1 - me), 64), sizes[t])

            def after(p, ds):
                def values():
                    r.mid[keys, lane(0)] += dot(p(), pair_rows(r.gmr[at_u, lane(0)]))

                def scores():
                    r.lo[keys, lane(0)] += dot(ds(), pair_rows(r.prv[at_u, lane(0)]))

                return [values, scores]

            return dict(
                size=sizes[t], off=off, after=after,
                q2=lambda: with_marks(pair_rows(r.prv[at_u, lane(0)]), both_rows(r.seg_qr[at_u, :])),
                do2=lambda: pair_rows(r.gmr[at_u, lane(0)]),
                lse=lambda: r.statsr[0, pl.ds(hp * tiles + t, 1), :],
                delta=lambda: r.statsr[1, pl.ds(hp * tiles + t, 1), :],
                k=lambda: with_marks(r.pv[keys, lane(width)], r.seg_k[keys, :]),
                v=lambda: r.pv[keys, lane(2 * width)],
            )

        grad_steps([[block(t, off) for t, off in offsets(group)] for group in groups])
        r.pv[:, lane(width)] = (r.lo[:, lane(0)] * (1.0 / LOG2E)).astype(BF16)
        r.pv[:, lane(2 * width)] = r.mid[:, lane(0)].astype(BF16)

    def own_pass(hp, _):
        own_queries(hp)
        ends_in_loop("own", hp, range(pairs))
        return 0

    lax.fori_loop(0, OUT_AFTER, own_pass, 0)
    for n, name in enumerate(BITS):
        pl.semaphore_signal(
            r.again.at[n], inc=1, device_id=partner_of(name, dp, blk, bits), device_id_type=MESH
        )

    for c, part in chunks(width, 256):
        grad = dot(r.ffn_t[...], r.ffn_in[:, c : c + part]).astype(BF16)
        for k in range(2):
            column_at = c + k * UNIT
            y, unit = column_at // (width // 2), column_at % (width // 2) // UNIT
            for d in range(16):
                put(unit, ORDERS[9], d, y, 0,
                    grad[d * block_rows : (d + 1) * block_rows, k * UNIT : (k + 1) * UNIT])
    for k in range(len(BITS)):
        pl.semaphore_wait(r.again.at[k], 1)
    red.start(out_chunk)
    ends("out", 0)
    lax.fori_loop(OUT_AFTER, pairs, own_pass, 0)

    send_gm.wait()
    send_stats.wait()
    r.pv[:, :width] = r.mixedv[...]

    def grad_qkv(j, order):
        columns = [pl.ds(aligned(y * (3 * width // 2) + j * UNIT, UNIT), UNIT) for y in range(2)]
        grad = dot(r.n1_t[...], jnp.concatenate([r.pv[:, at] for at in columns], 1)).astype(BF16)
        for y in range(2):
            for d in range(16):
                put(3 + j, order, d, y, 0,
                    grad[d * block_rows : (d + 1) * block_rows, y * UNIT : (y + 1) * UNIT])

    half_pairs = pairs // 2

    def first_pass(hp, _):
        other_queries(hp)
        grad_qkv(half_pairs + hp, ORDERS[10])

        @pl.when(hp == half_pairs - 1)
        def _():
            red.start(middle_chunk)

        ends_in_loop("oth", hp, range(half_pairs))
        return 0

    lax.fori_loop(0, half_pairs, first_pass, 0)

    def second_pass(hp, _):
        other_queries(hp)
        for k in range(2):
            grad_qkv(hp - half_pairs + 6 * k, ORDERS[11 + k])
            red.start(chunk_qkv(hp - half_pairs, k))
        ends_in_loop("oth", hp, range(half_pairs, pairs))
        return 0

    lax.fori_loop(half_pairs, pairs, second_pass, 0)

    load_w_qkv.wait()
    for c, part in chunks(width, 256):
        r.lo[:, c : c + part] = dot(r.pv[...], r.wa[c : c + part, : 3 * width], NT)
    ends("tail", 0)

    def norm_one_back(at):
        normed, inverse = standardize(r.xv[at, :].astype(F32))
        grad = r.lo[at, :]
        r.gains[8:16, :] += fold_sum(grad * normed)
        r.mid[at, :] = r.gf[at, :] + norm_backward(
            grad * row_of(r.gain_attn), normed, inverse
        )

    by_row_tiles(rows, norm_one_back)
    ends("tail", 1)
    out_gin = pltpu.make_async_copy(r.mid, r.input_grad, r.loads.at[8])
    out_gin.start()
    r.o_gains[0] = jnp.concatenate(
        [jnp.sum(r.gains[0:8, :], 0, keepdims=True), jnp.sum(r.gains[8:16, :], 0, keepdims=True),
         jnp.zeros((6, width), F32)], 0)

    def gain_copy(k):
        return pltpu.make_async_remote_copy(
            src_ref=r.o_gains.at[k], dst_ref=r.gains_in.at[k], send_sem=r.gain_sent.at[k], recv_sem=r.gain_got.at[k],
            device_id=partner_of(ORDER_A[k], dp, blk, bits), device_id_type=MESH)

    gain_copy(0).start()
    for k in range(5):
        ends("tail", 2 + k)
        gain_copy(k).wait()
        r.o_gains[k + 1] = r.o_gains[k] + r.gains_in[k]
        if k + 1 < 5:
            gain_copy(k + 1).start()
    ends("tail", 7)
    out_gin.wait()


def call_layer(x, seg, gain_attn, gain_ffn, w_qkv, w_out, w_up, w_down, cot):
    rows, width = x.shape
    ff = w_down.shape[0]
    tiles, pairs, block = rows // TILE, width // TILE, width // 16
    stat = (-(-pairs * tiles // 8) * 8, 2 * TILE)
    vmem = pl.BlockSpec(memory_space=pltpu.VMEM)
    anywhere = pl.BlockSpec(memory_space=pl.ANY)
    ins = dict(x=anywhere, seg=vmem, gain_attn=vmem, gain_ffn=vmem, w_qkv=anywhere, w_out=anywhere,
               w_up=anywhere, w_down=anywhere, cot=anywhere)
    outs = dict(
        layer_out=((rows, width), F32, anywhere), input_grad=((rows, width), F32, anywhere),
        o_gains=((6, 8, width), F32, vmem), o_qkv=((block, 3 * width // 2), F32, vmem),
        o_out=((block, width // 2), F32, vmem), o_up=((block, ff // 2), F32, vmem),
        o_down=((ff // 16, width // 2), F32, vmem),
    )
    big = ((rows, width), BF16)
    wide = ((rows, width), F32)
    scratch = dict(
        xv=big, xr=big, mixedv=big, cotv=big, pv=((rows, 3 * width), BF16), prv=((rows, 3 * width), BF16),
        wo=((width, width), BF16), wa=((width, ff), BF16), wb=((ff, width), BF16),
        mid=wide, lo=wide, gf=wide, ffn_in=big, ffn_t=((width, rows), BF16), act_t=((ff, rows), BF16),
        h=((rows, 512), F32), ga=((rows, 512), F32), act=((rows, 512), BF16), gh=((rows, 512), BF16),
        gmr=big, stats=((2,) + stat, F32), statsr=((2,) + stat, F32), top=(stat, F32), total=(stat, F32),
        segr=((1, rows), jnp.int32), seg_k=((rows, TILE), BF16), seg_q=((rows, TILE), BF16),
        seg_kr=((rows, TILE), BF16), seg_qr=((rows, TILE), BF16),
        gains=((16, width), F32), gains_in=((5, 8, width), F32),
        g=((24, 32, block, UNIT), BF16), recv=((24, 31, block, UNIT), BF16),
    )
    sems = dict(loads=(9,), sent=(5,), got=(5,), rs_sent=(17, 5), rs_got=(17, 5), gain_sent=(5,), gain_got=(5,))
    names = list(ins) + list(outs) + list(scratch) + list(sems) + ["again"]

    def body(*refs):
        r = dict(zip(names, refs))
        wb = r["wb"]
        extra = dict(
            kt=wb.at[0:width, 0:rows], ktr=wb.at[width : 2 * width, 0:rows],
            n1_t=wb.at[2 * width : 3 * width, 0:rows], gm=wb.at[3 * width : 3 * width + rows, :],
        )
        kernel_layer(list(r) + list(extra), *r.values(), *extra.values())

    return pl.pallas_call(
        body,
        out_shape=[jax.ShapeDtypeStruct(v[0], v[1]) for v in outs.values()],
        in_specs=list(ins.values()),
        out_specs=[v[2] for v in outs.values()],
        scratch_shapes=[pltpu.VMEM(*v) for v in scratch.values()]
        + [pltpu.SemaphoreType.DMA(n) for n in sems.values()]
        + [pltpu.SemaphoreType.REGULAR((len(BITS),))],
        compiler_params=pltpu.CompilerParams(
            collective_id=0, has_side_effects=True, vmem_limit_bytes=60 * 2**20
        ),
        name="layer",
    )(x, seg, gain_attn, gain_ffn, w_qkv, w_out, w_up, w_down, cot)


def padded(block, sides, width):
    for axis, dim in sides:
        count = lax.axis_size(axis)
        forward = [(i, i + 1) for i in range(count - 1)]
        backward = [(target, source) for source, target in forward]
        low = lax.ppermute(
            lax.slice_in_dim(block, block.shape[dim] - width, None, axis=dim), axis, forward
        )
        high = lax.ppermute(lax.slice_in_dim(block, 0, width, axis=dim), axis, backward)
        block = jnp.concatenate([low, block, high], axis=dim)
    return block


def from_behind(block, axis, distance):
    devices = range(lax.axis_size(axis))
    route = [(i - distance, i) for i in devices if i - distance in devices]
    return lax.ppermute(block, axis, route)


def normalize(values):
    centered = values - jnp.mean(values, -1, keepdims=True)
    variance = jnp.mean(centered * centered, -1, keepdims=True)
    inverse = lax.rsqrt(variance + 1e-05)
    return (centered * inverse, inverse)


def norm_back(grad_normed, normed, inverse):
    first = jnp.mean(grad_normed, -1, keepdims=True)
    second = jnp.mean(grad_normed * normed, -1, keepdims=True)
    return inverse * (grad_normed - first - normed * second)


def split_blocks(packed, seg_all):
    length = packed.shape[0]
    feature_count = packed.shape[1] // 2
    block_rows = math.gcd(length, 512)
    count_blocks = length // block_rows
    keys_blk = packed[:, :feature_count].reshape(
        count_blocks, block_rows, HEADS, feature_count // HEADS
    )
    vals_blk = packed[:, feature_count:].reshape(
        count_blocks, block_rows, HEADS, feature_count // HEADS
    )
    seg_blk = seg_all.reshape(count_blocks, block_rows)
    return (keys_blk, vals_blk, seg_blk)


def fetch_near(kv_local, seg_mark):
    return (
        padded(kv_local, (("blk", 0),), kv_local.shape[0]),
        padded(seg_mark, (("blk", 0),), kv_local.shape[0]),
    )


def block_scores(query_rows, keys_rows, seg_query, seg_keys):
    scale_factor = query_rows.shape[-1] ** (-0.5)
    scores = (
        jnp.einsum("qhd,khd->hqk", query_rows, keys_rows, preferred_element_type=jnp.float32)
        * scale_factor
    )
    allowed = (seg_query[:, None] == seg_keys[None, :])[None]
    return (jnp.where(allowed, scores, -1e30), allowed)


def attend_forward(query_rows, keys_blk, vals_blk, seg_blk, seg_query):
    row_count = query_rows.shape[0]

    def stats_step(carried, block_item):
        running, totals = carried
        scores, allowed = block_scores(query_rows, block_item[0], seg_query, block_item[1])
        newest = jnp.maximum(running, jnp.max(scores, -1))
        fresh = jnp.sum(jnp.where(allowed, jnp.exp(scores - newest[..., None]), 0.0), -1)
        return ((newest, totals * jnp.exp(running - newest) + fresh), None)

    start_max = jnp.full((HEADS, row_count), -1e30, jnp.float32)
    start_tot = jnp.zeros((HEADS, row_count), jnp.float32)
    (running, totals), unused = lax.scan(stats_step, (start_max, start_tot), (keys_blk, seg_blk))
    logsum = running + jnp.log(totals)

    def value_step(carried, block_item):
        scores, allowed = block_scores(query_rows, block_item[0], seg_query, block_item[2])
        prob_rows = jnp.where(allowed, jnp.exp(scores - logsum[..., None]), 0.0).astype(
            jnp.bfloat16
        )
        return (
            carried
            + jnp.einsum(
                "hqk,khd->qhd", prob_rows, block_item[1], preferred_element_type=jnp.float32
            ),
            None,
        )

    start_mix = jnp.zeros(query_rows.shape, jnp.float32)
    mixed, unused_two = lax.scan(value_step, start_mix, (keys_blk, vals_blk, seg_blk))
    return (mixed, logsum)


def attend_backward(
    query_rows, keys_blk, vals_blk, seg_blk, seg_query, logsum, grad_mixed, delta_rows
):
    scale_factor = query_rows.shape[-1] ** (-0.5)

    def grad_step(carried, block_item):
        keys_rows, vals_rows, seg_keys = block_item
        scores, allowed = block_scores(query_rows, keys_rows, seg_query, seg_keys)
        prob_rows = jnp.where(allowed, jnp.exp(scores - logsum[..., None]), 0.0)
        grad_vals = jnp.einsum(
            "hqk,qhd->khd",
            prob_rows.astype(jnp.bfloat16),
            grad_mixed,
            preferred_element_type=jnp.float32,
        )
        grad_probs = jnp.einsum(
            "qhd,khd->hqk", grad_mixed, vals_rows, preferred_element_type=jnp.float32
        )
        grad_scores = (prob_rows * (grad_probs - delta_rows[..., None])).astype(jnp.bfloat16)
        carried = (
            carried
            + jnp.einsum("hqk,khd->qhd", grad_scores, keys_rows, preferred_element_type=jnp.float32)
            * scale_factor
        )
        grad_keys = (
            jnp.einsum("hqk,qhd->khd", grad_scores, query_rows, preferred_element_type=jnp.float32)
            * scale_factor
        )
        return (carried, (grad_keys, grad_vals))

    start_grad = jnp.zeros(query_rows.shape, jnp.float32)
    grad_query, (grad_keys, grad_vals) = lax.scan(
        grad_step, start_grad, (keys_blk, vals_blk, seg_blk)
    )
    return (grad_query, grad_keys, grad_vals)


def per_device(tokens, segment_ids, gain_attn, w_qkv, w_out, gain_ffn, w_up, w_down, cotangent):
    inputs = tokens[0].astype(jnp.float32)
    seg_mark = segment_ids[0] + 1
    row_count, feature_count = inputs.shape
    head_size = feature_count // HEADS
    normed_one, inverse_one = normalize(inputs)
    attn_in = (normed_one * gain_attn).astype(jnp.bfloat16)
    projected = jnp.dot(attn_in, w_qkv, preferred_element_type=jnp.float32).astype(jnp.bfloat16)
    query_rows = projected[:, :feature_count].reshape(row_count, HEADS, head_size)
    kv_local = projected[:, feature_count:]
    packed, seg_near = fetch_near(kv_local, seg_mark)
    keys_blk, vals_blk, seg_blk = split_blocks(packed, seg_near)
    mixed, logsum = attend_forward(query_rows, keys_blk, vals_blk, seg_blk, seg_mark)
    mixed_b = mixed.reshape(row_count, feature_count).astype(jnp.bfloat16)
    middle = inputs + jnp.dot(mixed_b, w_out, preferred_element_type=jnp.float32)
    normed_two, inverse_two = normalize(middle)
    ffn_in = (normed_two * gain_ffn).astype(jnp.bfloat16)
    hidden = jnp.dot(ffn_in, w_up, preferred_element_type=jnp.float32)
    active, gelu_back = jax.vjp(partial(jax.nn.gelu, approximate=False), hidden)
    active_b = active.astype(jnp.bfloat16)
    layer_out = middle + jnp.dot(active_b, w_down, preferred_element_type=jnp.float32)
    upstream_b = cotangent[0]
    upstream = upstream_b.astype(jnp.float32)
    grad_down = jnp.einsum("nf,nd->fd", active_b, upstream_b, preferred_element_type=jnp.float32)
    grad_active = jnp.einsum("nd,fd->nf", upstream_b, w_down, preferred_element_type=jnp.float32)
    grad_hidden = gelu_back(grad_active)[0].astype(jnp.bfloat16)
    grad_up = jnp.einsum("nd,nf->df", ffn_in, grad_hidden, preferred_element_type=jnp.float32)
    grad_ffn_in = jnp.einsum("nf,df->nd", grad_hidden, w_up, preferred_element_type=jnp.float32)
    grad_gain_ffn = jnp.sum(grad_ffn_in * normed_two, 0)
    grad_middle = upstream + norm_back(grad_ffn_in * gain_ffn, normed_two, inverse_two)
    grad_branch = grad_middle.astype(jnp.bfloat16)
    grad_out = jnp.einsum("nd,ne->de", mixed_b, grad_branch, preferred_element_type=jnp.float32)
    grad_mixed = jnp.einsum(
        "ne,de->nd", grad_branch, w_out, preferred_element_type=jnp.float32
    ).astype(jnp.bfloat16)
    grad_mixed = grad_mixed.reshape(row_count, HEADS, head_size)
    delta_rows = jnp.einsum("qhd,qhd->hq", grad_mixed.astype(jnp.float32), mixed)
    grad_query, grad_keys, grad_vals = attend_backward(
        query_rows, keys_blk, vals_blk, seg_blk, seg_mark, logsum, grad_mixed, delta_rows
    )
    near_rows = 3 * row_count
    kv_terms = jnp.concatenate(
        [grad_keys.reshape(near_rows, feature_count), grad_vals.reshape(near_rows, feature_count)],
        1,
    )
    lower_rim = kv_terms[:row_count]
    own_rows = kv_terms[row_count : 2 * row_count]
    upper_rim = kv_terms[2 * row_count :]
    from_right = from_behind(lower_rim.astype(jnp.bfloat16), "blk", -1).astype(lower_rim.dtype)
    from_left = from_behind(upper_rim.astype(jnp.bfloat16), "blk", 1).astype(upper_rim.dtype)
    kv_home = own_rows + from_right + from_left
    grad_proj = jnp.concatenate([grad_query.reshape(row_count, feature_count), kv_home], 1).astype(
        jnp.bfloat16
    )
    grad_qkv = jnp.einsum("nd,ne->de", attn_in, grad_proj, preferred_element_type=jnp.float32)
    grad_attn_in = jnp.einsum("ne,de->nd", grad_proj, w_qkv, preferred_element_type=jnp.float32)
    grad_gain_attn = jnp.sum(grad_attn_in * normed_one, 0)
    input_grad = grad_middle + norm_back(grad_attn_in * gain_attn, normed_one, inverse_one)
    part_qkv, part_out, part_up, part_down, part_gain_attn, part_gain_ffn = (
        lax.psum_scatter(
            grad_qkv.astype(jnp.bfloat16), "dp", scatter_dimension=0, tiled=True
        ).astype(jnp.float32),
        lax.psum_scatter(
            grad_out.astype(jnp.bfloat16), "dp", scatter_dimension=0, tiled=True
        ).astype(jnp.float32),
        lax.psum_scatter(
            grad_up.astype(jnp.bfloat16), "dp", scatter_dimension=0, tiled=True
        ).astype(jnp.float32),
        lax.psum_scatter(
            grad_down.astype(jnp.bfloat16), "dp", scatter_dimension=0, tiled=True
        ).astype(jnp.float32),
        lax.psum_scatter(
            grad_gain_attn.astype(jnp.bfloat16), "dp", scatter_dimension=0, tiled=True
        ).astype(jnp.float32),
        lax.psum_scatter(
            grad_gain_ffn.astype(jnp.bfloat16), "dp", scatter_dimension=0, tiled=True
        ).astype(jnp.float32),
    )
    sum_qkv, sum_out, sum_up, sum_down = (
        lax.psum_scatter(
            part_qkv.astype(jnp.bfloat16), "blk", scatter_dimension=1, tiled=True
        ).astype(jnp.float32),
        lax.psum_scatter(
            part_out.astype(jnp.bfloat16), "blk", scatter_dimension=1, tiled=True
        ).astype(jnp.float32),
        lax.psum_scatter(
            part_up.astype(jnp.bfloat16), "blk", scatter_dimension=1, tiled=True
        ).astype(jnp.float32),
        lax.psum_scatter(
            part_down.astype(jnp.bfloat16), "blk", scatter_dimension=1, tiled=True
        ).astype(jnp.float32),
    )
    total_gain_attn, total_gain_ffn = lax.psum((part_gain_attn, part_gain_ffn), "blk")
    return (
        layer_out[None],
        input_grad[None],
        total_gain_attn,
        sum_qkv,
        sum_out,
        total_gain_ffn,
        sum_up,
        sum_down,
    )


def copy_kernel(count, *refs):
    source, target, held = refs[:count], refs[count : 2 * count], refs[2 * count : 3 * count]
    sems = refs[3 * count]
    loads = [pltpu.make_async_copy(source[k], held[k], sems.at[0, k]) for k in range(count)]
    stores = [pltpu.make_async_copy(held[k], target[k], sems.at[1, k]) for k in range(count)]
    for copy in loads:
        copy.start()
    for load, store in zip(loads, stores):
        load.wait()
        store.start()
    for copy in stores:
        copy.wait()


def copy_out(arrays):
    anywhere = pl.BlockSpec(memory_space=pl.ANY)
    return pl.pallas_call(
        partial(copy_kernel, len(arrays)),
        out_shape=[jax.ShapeDtypeStruct(a.shape, a.dtype) for a in arrays],
        in_specs=[anywhere] * len(arrays),
        out_specs=[anywhere] * len(arrays),
        scratch_shapes=[pltpu.VMEM(a.shape, a.dtype) for a in arrays]
        + [pltpu.SemaphoreType.DMA((2, len(arrays)))],
        name="copy_out",
    )(*arrays)


def fast(tokens, segment_ids, gain_attn, w_qkv, w_out, gain_ffn, w_up, w_down, cotangent):
    x, cot = tokens[0], cotangent[0]
    rows, width = x.shape
    layer_out, input_grad, gains, g_qkv, g_out, g_up, g_down = call_layer(
        x, segment_ids, gain_attn.reshape(-1, TILE), gain_ffn.reshape(-1, TILE), w_qkv, w_out, w_up, w_down, cot
    )
    layer_out, input_grad, g_qkv, g_out, g_up, g_down = copy_out(
        [layer_out, input_grad, g_qkv, g_out, g_up, g_down]
    )
    block = width // 16
    mine = lax.dynamic_slice(gains[5], (0, lax.axis_index("dp") * block), (2, block))
    return (layer_out[None], input_grad[None], mine[1], g_qkv, g_out, mine[0], g_up, g_down)


def fits(mesh, tokens, w_qkv, w_up):
    rows, width, ff = tokens.shape[1] // mesh.shape["blk"], tokens.shape[2], w_up.shape[1]
    return (
        mesh.shape["dp"] == 16 and mesh.shape["blk"] == 2 and tokens.shape[0] == 16
        and rows % TILE == 0 and rows <= 640 and (rows - min(rows, REACH)) % 64 == 0
        and width == HEADS * 64 and ff == 4 * width
    )


def solution(mesh):
    def program(*args):
        body = fast if fits(mesh, args[0], args[3], args[6]) else per_device
        rows, whole = P("dp", "blk", None), P()
        return jax.shard_map(
            body,
            mesh=mesh,
            in_specs=(rows, P("dp", "blk"), whole, whole, whole, whole, whole, whole, rows),
            out_specs=(rows, rows, P("dp"), P("dp", "blk"), P("dp", "blk"), P("dp"), P("dp", "blk"), P("dp", "blk")),
            check_vma=False,
        )(*args)

    return program
```
